128 devices in a mesh: px: 8 (over z, core), py: 16 (over x, y).
Axes of the slice: x: 4, y: 4, z: 4, core: 2. Of those that a mesh axis runs over, the one named last changes fastest.
Arguments:
- a_blocks: bfloat16 [12288, 27, 4096], P(('px', 'py')), may hold values from -1.5 to 1.5
- p_blocks: bfloat16 [12288, 4096], P(('px', 'py')), may hold values from -0.75 to 0.75
- a_source: int32 [12288, 27], P(('px', 'py')), may hold values from 0 to 1119, as said below
- send_list: int32 [128, 128, 8], P(('px', 'py')), may hold values from -1 to 95, as said below
- agg_local: int32 [12288], P(('px', 'py')), may hold values from 0 to 15, as said below
- coarse_slot: int32 [12288, 27], P(('px', 'py')), may hold values from 0 to 26
- coarse_target: int32 [2048], P(('px', 'py')), may hold values from 0 to 2047, as said below
Outputs:
- coarse: bfloat16 [2048, 27, 4096], P(('px', 'py'))
The draws below stay inside these ranges and needn't reach their ends.
Inputs may be any that keep to these rules, and one draw needn't show every extreme that they name: `a_source`: column 0 of a row is the row itself. An entry of 96 or more names a slot received from device (entry - 96) // 8, slot (entry - 96) % 8, which that device fills; every filled slot is named by some entry of the receiving device. `send_list`: filled slots from one sender to one receiver come first; no device sends to itself; each device fills all 8 slots for the device after it in px+py order; row 95 is sent in every draw. `agg_local`: each of a device's 16 agglomerates holds exactly 6 of its elements. `coarse_target`: A permutation of the coarse rows; the rows formed on a device go to devices with the same px index; at most 2 go from one device to one device, and in every draw exactly 2 for each pair that is used.
All inputs are finite; a program needn't handle non-finite values.
Results may differ from the reference program's by a relative error of at most 0.0049.
Values may be sent and summed in bfloat16 or wider, within the bound.
A program may use at most 384 MiB of HBM per device.

```python
import jax
import jax.numpy as jnp
from jax import lax

B = 64
NB = 96
K = 27
S = 27
AGG = 6
Q = 8
CCAP = 2
XDEV = 8
YDEV = 16
ALLDEV = 128
NCL = 16
ROWS = 12288
COARSE = 2048


def ghost_pattern(key):
    count_key, row_key, ref_key = jax.random.split(jax.random.fold_in(key, 7), 3)
    counts = jax.random.randint(count_key, (ALLDEV, ALLDEV), 0, Q + 1)
    device_ids = jnp.arange(ALLDEV)
    counts = jnp.where(device_ids[:, None] == device_ids[None, :], 0, counts)
    following = (device_ids[:, None] + 1) % ALLDEV == device_ids[None, :]
    counts = jnp.where(following, Q, counts)
    slot_ids = jnp.arange(Q)
    filled = slot_ids[None, None, :] < counts[:, :, None]
    rows_sent = jax.random.randint(row_key, (ALLDEV, ALLDEV, Q), 0, NB)
    rows_sent = rows_sent.at[0, 1 % ALLDEV, 0].set(NB - 1)
    sending = jnp.where(filled, rows_sent, -1)
    positions = NB * (K - 1)

    def receiver(device):
        sub_key = jax.random.fold_in(ref_key, device)
        perm_key, pick_key, local_key, coin_key = jax.random.split(sub_key, 4)
        active = filled[:, device, :].reshape(-1)
        active_count = jnp.sum(active.astype(jnp.int32))
        slot_order = jnp.argsort(jnp.where(active, 0, 1), stable=True)
        turns = jnp.arange(positions)
        picked = jax.random.randint(pick_key, (positions,), 0, 1 << 30) % active_count
        any_slot = slot_order[picked]
        first_slot = slot_order[jnp.minimum(turns, ALLDEV * Q - 1)]
        local_rows = jax.random.randint(local_key, (positions,), 0, NB)
        coins = jax.random.randint(coin_key, (positions,), 0, 4)
        extra = jnp.where(coins == 0, NB + any_slot, local_rows)
        values = jnp.where(turns < active_count, NB + first_slot, extra)
        places = jax.random.permutation(perm_key, positions)
        refs = jnp.zeros((positions,), jnp.int32).at[places].set(values.astype(jnp.int32))
        own = jnp.arange(NB, dtype=jnp.int32)[:, None]
        return jnp.concatenate([own, refs.reshape(NB, K - 1)], axis=1)
    sources = jax.vmap(receiver)(jnp.arange(ALLDEV))
    return (sending.astype(jnp.int32), sources.reshape(ALLDEV * NB, K).astype(jnp.int32))


def draw_a_source(key, part):
    return ghost_pattern(key)[1]


def draw_send_list(key, part):
    return ghost_pattern(key)[0]


def draw_agg_local(key, part):

    def one_device(device):
        return jax.random.permutation(jax.random.fold_in(key, device), NB) // AGG
    return jax.vmap(one_device)(jnp.arange(ALLDEV)).reshape(-1).astype(jnp.int32)


def draw_coarse_target(key, part):
    shift_key, order_key = jax.random.split(jax.random.fold_in(key, 11))
    used = NCL // CCAP

    def group(xrow):
        shifts = jax.random.permutation(jax.random.fold_in(shift_key, xrow), YDEV)[:used]

        def source(ypos):
            local = jnp.arange(NCL)
            unit = local // CCAP
            within = local % CCAP
            dest_y = (ypos + shifts[unit]) % YDEV
            target = (xrow * YDEV + dest_y) * NCL + unit * CCAP + within
            order = jax.random.permutation(jax.random.fold_in(order_key, xrow * YDEV + ypos), NCL)
            return target[order]
        return jax.vmap(source)(jnp.arange(YDEV))
    return jax.vmap(group)(jnp.arange(XDEV)).reshape(-1).astype(jnp.int32)


def with_ends(values, stream_key, low, largest):
    longest = values.shape.index(max(values.shape))
    spots = []
    for shift in (0, 1):
        where = [jax.random.randint(jax.random.fold_in(stream_key, axis), (), 0, length) for axis, length in enumerate(values.shape)]
        where[longest] = (where[longest] + shift) % values.shape[longest]
        spots.append(tuple(where))
    return values.at[spots[0]].set(low).at[spots[1]].set(largest)


def level_of(stream_key, extent, cuts, smallest, high):
    def one(position, parts):
        steps = jax.random.uniform(jax.random.fold_in(jax.random.fold_in(stream_key, 6), position), (parts,), jnp.float32, smallest / len(cuts), high / len(cuts))
        return jnp.repeat(jnp.exp(steps), extent[position] // parts).reshape((-1,) + (1,) * (len(extent) - position - 1))

    level = one(*cuts[0])
    for cut in cuts[1:]:
        level = level * one(*cut)
    return level


def gaussian(key, shape, width, limit, shards=(), held_as=jnp.bfloat16):
    factor_of = level_of(key, shape, shards, -0.22, 0.18) if shards else 1.0
    entries = jax.random.normal(key, shape, jnp.float32) * width * factor_of
    return jnp.minimum(jnp.maximum(entries, -limit), limit).astype(held_as)


def setup_inputs(seed: int = 0) -> dict:
    splits = jax.random.split(jax.random.key(seed), 8)
    return {
        "a_blocks": gaussian(splits[0], (ROWS, K, B * B), 0.25, 1.5, ((0, 128),)),
        "p_blocks": gaussian(splits[1], (ROWS, B * B), B ** -0.5, 0.75, ((0, 128),)),
        "a_source": draw_a_source(jax.random.fold_in(splits[7], 71), 0),
        "send_list": draw_send_list(jax.random.fold_in(splits[7], 71), 0),
        "agg_local": draw_agg_local(jax.random.fold_in(splits[7], 71), 0),
        "coarse_slot": with_ends(jax.random.randint(splits[5], (ROWS, K), 0, S), jax.random.fold_in(splits[5], 1), 0, S - 1).astype(jnp.int32),
        "coarse_target": draw_coarse_target(jax.random.fold_in(splits[7], 71), 0),
    }


def reference(a_blocks, p_blocks, a_source, send_list, agg_local, coarse_slot, coarse_target):
    flat_size = B * B

    def one_device(device):
        start = device * NB
        a_rows = lax.dynamic_slice_in_dim(a_blocks, start, NB, 0)
        p_rows = lax.dynamic_slice_in_dim(p_blocks, start, NB, 0)
        sources = lax.dynamic_slice_in_dim(a_source, start, NB, 0)
        groups = lax.dynamic_slice_in_dim(agg_local, start, NB, 0)
        slots = lax.dynamic_slice_in_dim(coarse_slot, start, NB, 0)
        ghost = jnp.maximum(sources - NB, 0)
        sender = (ghost // Q).astype(jnp.int32)
        slot_in = (ghost % Q).astype(jnp.int32)
        sent_row = send_list[sender, device, slot_in]
        is_local = sources < NB
        global_row = jnp.where(is_local, start + sources, sender * NB + sent_row)
        filled = is_local | (sent_row >= 0)
        columns = p_blocks[jnp.maximum(global_row, 0).astype(jnp.int32)]
        columns = jnp.where(filled[:, :, None], columns, jnp.zeros_like(columns))
        a_split = a_rows.reshape(NB, K, B, B).astype(jnp.float32)
        col_split = columns.reshape(NB, K, B, B).astype(jnp.float32)
        product = jnp.einsum("gkij,gkjl->gkil", a_split, col_split).astype(jnp.bfloat16)
        own_split = p_rows.reshape(NB, B, B).astype(jnp.float32)
        triple = jnp.einsum("gia,gkil->gkal", own_split, product.astype(jnp.float32))
        segment_ids = (groups[:, None] * S + slots).reshape(-1).astype(jnp.int32)
        summed = jax.ops.segment_sum(triple.reshape(NB * K, flat_size), segment_ids, num_segments=NCL * S)
        return summed.astype(jnp.bfloat16).reshape(NCL, S, flat_size)

    partials = lax.map(one_device, jnp.arange(ALLDEV, dtype=jnp.int32))
    flat_rows = partials.reshape(COARSE, S, flat_size)
    result = jnp.zeros_like(flat_rows).at[coarse_target.astype(jnp.int32)].set(flat_rows)
    return result
```

```python
import jax
import jax.numpy as jnp
from jax import lax
from jax.experimental import pallas as pl
from jax.experimental.pallas import tpu as pltpu
from jax.sharding import PartitionSpec as P

B = 64
L = 2 * B
NB = 96
K = 27
S = 27
AGG = 6
Q = 8
CCAP = 2
NCL = NB // AGG
PEERS = 128
DEST = NCL * S
GROUP = 4
TILES = PEERS * Q // 2
LOCAL = NB + 2
GROUPS = 1024
POSITIONS = GROUPS * GROUP
CHUNK = 64
BATCH = 16
STEPS = GROUPS // CHUNK
ROWS_STEP = 16
F32 = jnp.float32
BF16 = jnp.bfloat16


def low_lanes(shape):
    return lax.broadcasted_iota(jnp.int32, shape, 1) < B


def params(limit):
    return pltpu.CompilerParams(
        dimension_semantics=("arbitrary",), vmem_limit_bytes=limit * 1024 * 1024
    )


def pack_kernel(wanted, p_ref, send_ref, local_ref, wide):
    step = pl.program_id(0)

    @pl.when(step == 0)
    def _():
        low = low_lanes((ROWS_STEP, L))

        def relayout(group, carry):
            row = pl.multiple_of(group * ROWS_STEP, ROWS_STEP)
            for m in range(B // 2):
                both = p_ref[pl.ds(row, ROWS_STEP), pl.ds(m * L, L)].astype(F32)
                turned = pltpu.roll(both, B, 1)
                even = jnp.where(low, both, turned)
                odd = jnp.where(low, turned, both)
                wide[pl.ds(2 * m, ROWS_STEP, stride=B), :] = even
                wide[pl.ds(2 * m + 1, ROWS_STEP, stride=B), :] = odd
            for g in range(ROWS_STEP):
                local_ref[row + g] = wide[pl.ds(g * B, B), :].astype(BF16)
            return carry

        lax.fori_loop(0, NB // ROWS_STEP, relayout, 0)
        zero = jnp.zeros((B, L), BF16)
        local_ref[NB] = zero
        local_ref[NB + 1] = zero

    low = low_lanes((B, L))
    per_step = send_ref.shape[0]

    def fill(tile, carry):
        slot = 2 * (step * per_step + tile)
        first = wanted[slot]
        second = wanted[slot + 1]
        first = jnp.where(first < 0, NB, first)
        second = jnp.where(second < 0, NB, second)
        send_ref[tile] = jnp.where(low, local_ref[first], local_ref[second])
        return carry

    lax.fori_loop(0, per_step, fill, 0, unroll=8)


def pack(wanted, p_blocks):
    per_step = TILES // 8
    return pl.pallas_call(
        pack_kernel,
        grid_spec=pltpu.PrefetchScalarGridSpec(
            num_scalar_prefetch=1,
            grid=(TILES // per_step,),
            in_specs=[pl.BlockSpec((NB, B * B), lambda i, w: (0, 0))],
            out_specs=[
                pl.BlockSpec((per_step, B, L), lambda i, w: (i, 0, 0)),
                pl.BlockSpec((LOCAL, B, L), lambda i, w: (0, 0, 0)),
            ],
            scratch_shapes=[pltpu.VMEM((ROWS_STEP * B, L), F32)],
        ),
        out_shape=[
            jax.ShapeDtypeStruct((TILES, B, L), BF16),
            jax.ShapeDtypeStruct((LOCAL, B, L), BF16),
        ],
        compiler_params=params(24),
        name="pack",
    )(wanted, p_blocks)


def left_kernel(
    dest_in, code_in, a_ref, p_ref, sorted_hbm, code_ref, group_ref, count_ref,
    held, wide, turned_p, cursor, sem,
):
    step = pl.program_id(0)

    @pl.when(step == 0)
    def _():
        def clear(d, carry):
            cursor[d] = 0
            return carry

        lax.fori_loop(0, DEST, clear, 0, unroll=8)

        def count(e, carry):
            d = dest_in[e]
            cursor[d] = cursor[d] + 1
            return carry

        lax.fori_loop(0, NB * K, count, 0, unroll=8)

        def place(d, at):
            here = cursor[d]
            cursor[d] = at
            return at + ((here + GROUP - 1) // GROUP) * GROUP

        total = lax.fori_loop(0, DEST, place, 0, unroll=8)
        count_ref[0] = total // GROUP

        def blank(i, carry):
            code_ref[i] = 2 * NB
            return carry

        lax.fori_loop(0, POSITIONS, blank, 0, unroll=16)

        def nowhere(i, carry):
            group_ref[i] = DEST
            return carry

        lax.fori_loop(0, GROUPS, nowhere, 0, unroll=16)
        zero = jnp.zeros((B, L), BF16)

        def wipe(i, carry):
            held[i] = zero
            return carry

        lax.fori_loop(0, 2 * GROUPS, wipe, 0, unroll=16)

    for g in range(ROWS_STEP):
        turned_p[g] = p_ref[g].astype(F32).T[:B].astype(BF16)

    low16 = low_lanes((ROWS_STEP, L))
    lane = lax.broadcasted_iota(jnp.int32, (B, L), 1)
    low = lane < B
    half = jnp.where(low, 0, 1)

    def insert(row, k, value, valid):
        e = (step * ROWS_STEP + row) * K + k
        d = dest_in[e]
        at = cursor[d]
        cursor[d] = at + valid
        at = jnp.where(valid == 1, at, POSITIONS)
        code_ref[at] = code_in[e]
        group_ref[at // GROUP] = d
        tile = at // 2
        held[tile] = jnp.where(half == at % 2, value, held[tile].astype(F32)).astype(BF16)

    def pair_step(pair, carry):
        first = 2 * pair
        valid = jnp.where(first + 1 < K, 1, 0)
        second = jnp.minimum(first + 1, K - 1)
        for m in range(B // 2):
            one = a_ref[first, :, pl.ds(m * L, L)].astype(F32)
            two = a_ref[second, :, pl.ds(m * L, L)].astype(F32)
            wide[pl.ds(2 * m, ROWS_STEP, stride=B), :] = jnp.where(
                low16, one, pltpu.roll(two, B, 1)
            )
            wide[pl.ds(2 * m + 1, ROWS_STEP, stride=B), :] = jnp.where(
                low16, pltpu.roll(one, B, 1), two
            )
        for row in range(ROWS_STEP):
            block = wide[pl.ds(row * B, B), :].astype(BF16)
            value = jnp.dot(turned_p[row], block, preferred_element_type=F32)
            turned = pltpu.roll(value, B, 1)
            insert(row, first, jnp.where(low, value, turned), 1)
            insert(row, second, jnp.where(low, turned, value), valid)
        return carry

    lax.fori_loop(0, (K + 1) // 2, pair_step, 0)

    @pl.when(step == pl.num_programs(0) - 1)
    def _():
        copy = pltpu.make_async_copy(held.at[pl.ds(0, 2 * GROUPS)], sorted_hbm, sem)
        copy.start()
        copy.wait()


def left(dest, code, a_turned, local):
    return pl.pallas_call(
        left_kernel,
        grid_spec=pltpu.PrefetchScalarGridSpec(
            num_scalar_prefetch=2,
            grid=(NB // ROWS_STEP,),
            in_specs=[
                pl.BlockSpec((K, ROWS_STEP, B * B), lambda i, *_: (0, i, 0)),
                pl.BlockSpec((ROWS_STEP, B, L), lambda i, *_: (i, 0, 0)),
            ],
            out_specs=[
                pl.BlockSpec(memory_space=pl.ANY),
                pl.BlockSpec(memory_space=pltpu.SMEM),
                pl.BlockSpec(memory_space=pltpu.SMEM),
                pl.BlockSpec(memory_space=pltpu.SMEM),
            ],
            scratch_shapes=[
                pltpu.VMEM((2 * GROUPS + 1, B, L), BF16),
                pltpu.VMEM((ROWS_STEP * B, L), F32),
                pltpu.VMEM((ROWS_STEP, B, B), BF16),
                pltpu.SMEM((DEST,), jnp.int32),
                pltpu.SemaphoreType.DMA,
            ],
        ),
        out_shape=[
            jax.ShapeDtypeStruct((2 * GROUPS, B, L), BF16),
            jax.ShapeDtypeStruct((POSITIONS + GROUP,), jnp.int32),
            jax.ShapeDtypeStruct((GROUPS + 1,), jnp.int32),
            jax.ShapeDtypeStruct((1,), jnp.int32),
        ],
        compiler_params=params(56),
        cost_estimate=pl.CostEstimate(
            flops=2 * NB * K * B**3 * 16, bytes_accessed=60_000_000, transcendentals=0
        ),
        name="left",
    )(dest, code, a_turned, local)


def right_kernel(
    code_ref, group_ref, count_ref, bucket_ref, t_ref, local_hbm, ghost_hbm, out_ref,
    blocks, total, wide, halves, sems,
):
    step = pl.program_id(0)
    groups = count_ref[0]

    @pl.when(step == 0)
    def _():
        mine = pltpu.make_async_copy(local_hbm, blocks.at[pl.ds(0, LOCAL)], sems.at[0])
        others = pltpu.make_async_copy(ghost_hbm, blocks.at[pl.ds(LOCAL, TILES)], sems.at[1])
        mine.start()
        others.start()
        low = low_lanes((B, L))
        halves[0] = jnp.where(low, 1.0, 0.0).astype(BF16)
        halves[1] = jnp.where(low, 0.0, 1.0).astype(BF16)
        zero = jnp.zeros((B, L), F32)

        def clear(i, carry):
            total[i] = zero
            return carry

        lax.fori_loop(0, DEST + 1, clear, 0, unroll=8)
        mine.wait()
        others.wait()

    @pl.when(step < STEPS)
    def _():
        def batch(b, carry):
            for u in range(BATCH):
                here = b * BATCH + u
                group = step * CHUNK + here
                lhs = jnp.concatenate([t_ref[2 * here], t_ref[2 * here + 1]], axis=1)
                parts = []
                for w in range(GROUP):
                    code = code_ref[group * GROUP + w]
                    parts.append(blocks[code // 2] * halves[code % 2])
                rhs = jnp.concatenate(parts, axis=0)
                d = group_ref[group]
                total[d] += jnp.dot(lhs, rhs, preferred_element_type=F32)
            return carry

        left_over = groups - step * CHUNK
        batches = jnp.clip((left_over + BATCH - 1) // BATCH, 0, CHUNK // BATCH)
        lax.fori_loop(0, batches, batch, 0)

    @pl.when(step >= STEPS)
    def _():
        base = (step - STEPS) * S
        low = low_lanes((B // 2, L))

        def emit(part, carry):
            for u in range(9):
                s = part * 9 + u
                value = total[base + s]
                wide[pl.ds(u * B, B), :] = value + pltpu.roll(value, B, 1)
                even = wide[pl.ds(u * B, B // 2, stride=2), :]
                odd = wide[pl.ds(u * B + 1, B // 2, stride=2), :]
                out_ref[0, s] = jnp.where(low, even, odd).astype(BF16)
            return carry

        lax.fori_loop(0, S // 9, emit, 0)


def right(code, group, count, bucket, ordered, local, ghost, peers_y):
    last = STEPS - 1

    def t_map(i, code_ref, group_ref, count_ref, bucket_ref):
        used = jnp.maximum((count_ref[0] + CHUNK - 1) // CHUNK - 1, 0)
        return (jnp.minimum(jnp.minimum(i, last), used), 0, 0)

    def out_map(i, code_ref, group_ref, count_ref, bucket_ref):
        return (bucket_ref[jnp.maximum(i - STEPS, 0)], 0, 0, 0)

    return pl.pallas_call(
        right_kernel,
        grid_spec=pltpu.PrefetchScalarGridSpec(
            num_scalar_prefetch=4,
            grid=(STEPS + NCL,),
            in_specs=[
                pl.BlockSpec((2 * CHUNK, B, L), t_map),
                pl.BlockSpec(memory_space=pl.ANY),
                pl.BlockSpec(memory_space=pl.ANY),
            ],
            out_specs=pl.BlockSpec((1, S, B // 2, L), out_map),
            scratch_shapes=[
                pltpu.VMEM((LOCAL + TILES, B, L), BF16),
                pltpu.VMEM((DEST + 1, B, L), F32),
                pltpu.VMEM((9 * B, L), F32),
                pltpu.VMEM((2, B, L), BF16),
                pltpu.SemaphoreType.DMA((2,)),
            ],
        ),
        out_shape=jax.ShapeDtypeStruct((peers_y * CCAP, S, B // 2, L), BF16),
        compiler_params=params(48),
        name="right",
    )(code, group, count, bucket, ordered, local, ghost)


def place_kernel(from_ref, in_ref, out_ref, wide):
    step = pl.program_id(0)
    span = NCL * B // 2

    @pl.when(step < NCL)
    def _():
        for s in range(S):
            wide[pl.ds(s * span + step, B // 2, stride=NCL), :] = in_ref[0, s].astype(F32)

    @pl.when(step >= NCL)
    def _():
        def flatten(u, carry):
            start = pl.multiple_of(((step - NCL) * 9 + u) * span, span)
            for m in range(B // 2):
                out_ref[u, :, pl.ds(m * L, L)] = wide[
                    pl.ds(start + m * NCL, NCL), :
                ].astype(BF16)
            return carry

        lax.fori_loop(0, 9, flatten, 0)


def place(origin, arrived):
    return pl.pallas_call(
        place_kernel,
        grid_spec=pltpu.PrefetchScalarGridSpec(
            num_scalar_prefetch=1,
            grid=(NCL + S // 9,),
            in_specs=[
                pl.BlockSpec(
                    (1, S, B // 2, L), lambda i, o: (o[jnp.minimum(i, NCL - 1)], 0, 0, 0)
                )
            ],
            out_specs=pl.BlockSpec((9, NCL, B * B), lambda i, o: (jnp.maximum(i - NCL, 0), 0, 0)),
            scratch_shapes=[pltpu.VMEM((S * NCL * B // 2, L), F32)],
        ),
        out_shape=jax.ShapeDtypeStruct((S, NCL, B * B), BF16),
        compiler_params=params(32),
        name="place",
    )(origin, arrived)


def lists(a_source, agg_local, coarse_slot):
    dest = (agg_local[:, None] * S + coarse_slot).reshape(-1)
    ghost = a_source - NB + 2 * LOCAL
    code = jnp.where(a_source < NB, 2 * a_source, ghost).reshape(-1)
    return dest, code


def routes(targets, me):
    column = targets // NCL % targets.shape[0]
    order = jnp.arange(NCL)
    same = column[:, :, None] == column[:, None, :]
    earlier = order[None, None, :] < order[None, :, None]
    rank = jnp.sum((same & earlier).astype(jnp.int32), axis=2)
    source = jnp.arange(targets.shape[0])[:, None] * CCAP + rank
    here = (column == me)[:, :, None] & ((targets % NCL)[:, :, None] == order[None, None, :])
    origin = jnp.sum(jnp.where(here, source[:, :, None], 0), axis=(0, 1))
    bucket = (column * CCAP + rank)[me]
    return bucket.astype(jnp.int32), origin.astype(jnp.int32)


def body(a_blocks, p_blocks, a_source, send_list, agg_local, coarse_slot, coarse_target):
    peers_y = lax.axis_size("py")
    me = lax.axis_index("py")
    sending, local = pack(send_list.reshape(-1), p_blocks)
    ghost = lax.all_to_all(
        sending.reshape(PEERS, Q // 2 * B, L), ("px", "py"), split_axis=0, concat_axis=0, tiled=True
    ).reshape(TILES, B, L)
    targets = lax.all_gather(coarse_target, "py")
    bucket, origin = routes(targets, me)
    dest, code = lists(a_source, agg_local, coarse_slot)
    ordered, code, group, count = left(dest, code, a_blocks.transpose(1, 0, 2), local)
    rows = right(code, group, count, bucket, ordered, local, ghost, peers_y)
    arrived = lax.all_to_all(
        rows.reshape(peers_y, CCAP * S * B // 2, L), "py", split_axis=0, concat_axis=0, tiled=True
    ).reshape(peers_y * CCAP, S, B // 2, L)
    return place(origin, arrived).transpose(1, 0, 2)


def solution(mesh):
    both = ("px", "py")
    in_specs = (
        P(both, None, None), P(both, None), P(both, None), P(both, None, None), P(both),
        P(both, None), P(both),
    )
    return jax.shard_map(
        body, mesh=mesh, in_specs=in_specs, out_specs=P(both, None, None), check_vma=False
    )
```

```python
import jax
import jax.numpy as jnp
from jax import lax
from jax.experimental import pallas as pl
from jax.experimental.pallas import tpu as pltpu
from jax.sharding import PartitionSpec as P

B = 64
L = 2 * B
NB = 96
K = 27
S = 27
AGG = 6
Q = 8
CCAP = 2
NCL = NB // AGG
PEERS = 128
DEST = NCL * S
GROUP = 4
TILES = PEERS * Q // 2
LOCAL = NB + 2
GROUPS = 1024
POSITIONS = GROUPS * GROUP
CHUNK = 128
PITCH = 72
SPAN = Q // 2 * B
NOTE = 8
BATCH = 16
STEPS = GROUPS // CHUNK
ROWS_STEP = 16
F32 = jnp.float32
BF16 = jnp.bfloat16


def low_lanes(shape):
    return lax.broadcasted_iota(jnp.int32, shape, 1) < B


def params(limit):
    return pltpu.CompilerParams(
        dimension_semantics=("arbitrary",), vmem_limit_bytes=limit * 1024 * 1024
    )


def pack_kernel(wanted, p_ref, note_ref, send_ref, local_ref, wide):
    step = pl.program_id(0)

    @pl.when(step == 0)
    def _():
        low = low_lanes((ROWS_STEP, L))

        def relayout(group, carry):
            row = pl.multiple_of(group * ROWS_STEP, ROWS_STEP)
            for m in range(B // 2):
                both = p_ref[pl.ds(row, ROWS_STEP), pl.ds(m * L, L)].astype(F32)
                turned = pltpu.roll(both, B, 1)
                even = jnp.where(low, both, turned)
                odd = jnp.where(low, turned, both)
                wide[pl.ds(2 * m, ROWS_STEP, stride=PITCH), :] = even
                wide[pl.ds(2 * m + 1, ROWS_STEP, stride=PITCH), :] = odd
            for g in range(ROWS_STEP):
                local_ref[row + g] = wide[pl.ds(g * PITCH, B), :].astype(BF16)
            return carry

        lax.fori_loop(0, NB // ROWS_STEP, relayout, 0)
        zero = jnp.zeros((B, L), BF16)
        local_ref[NB] = zero
        local_ref[NB + 1] = zero

    low = low_lanes((B, L))
    per_step = send_ref.shape[0]

    def fill(peer, carry):
        for u in range(Q // 2):
            slot = (step * per_step + peer) * Q + 2 * u
            first = wanted[slot]
            second = wanted[slot + 1]
            first = jnp.where(first < 0, NB, first)
            second = jnp.where(second < 0, NB, second)
            send_ref[peer, u * B : (u + 1) * B] = jnp.where(
                low, local_ref[first], local_ref[second]
            )
        send_ref[peer, SPAN:] = note_ref[...]
        return carry

    lax.fori_loop(0, per_step, fill, 0, unroll=2)


def pack(wanted, p_blocks, note):
    per_step = PEERS // 8
    return pl.pallas_call(
        pack_kernel,
        grid_spec=pltpu.PrefetchScalarGridSpec(
            num_scalar_prefetch=1,
            grid=(PEERS // per_step,),
            in_specs=[
                pl.BlockSpec((NB, B * B), lambda i, w: (0, 0)),
                pl.BlockSpec((NOTE, L), lambda i, w: (0, 0)),
            ],
            out_specs=[
                pl.BlockSpec((per_step, SPAN + NOTE, L), lambda i, w: (i, 0, 0)),
                pl.BlockSpec((LOCAL, B, L), lambda i, w: (0, 0, 0)),
            ],
            scratch_shapes=[pltpu.VMEM((ROWS_STEP * PITCH, L), F32)],
        ),
        out_shape=[
            jax.ShapeDtypeStruct((PEERS, SPAN + NOTE, L), BF16),
            jax.ShapeDtypeStruct((LOCAL, B, L), BF16),
        ],
        compiler_params=params(60),
        name="pack",
    )(wanted, p_blocks, note)


def left_kernel(
    dest_in, code_in, a_ref, p_ref, sorted_hbm, code_ref, group_ref, count_ref,
    held, wide, turned_p, cursor, sem,
):
    step = pl.program_id(0)

    @pl.when(step == 0)
    def _():
        def clear(d, carry):
            cursor[d] = 0
            return carry

        lax.fori_loop(0, DEST, clear, 0, unroll=8)

        def count(e, carry):
            d = dest_in[e]
            cursor[d] = cursor[d] + 1
            return carry

        lax.fori_loop(0, NB * K, count, 0, unroll=8)

        def place(d, at):
            here = cursor[d]
            cursor[d] = at
            return at + ((here + GROUP - 1) & -GROUP)

        total = lax.fori_loop(0, DEST, place, 0, unroll=8)
        count_ref[0] = total >> 2

        def blank(i, carry):
            code_ref[i] = 2 * NB
            return carry

        lax.fori_loop(0, POSITIONS, blank, 0, unroll=16)

        def nowhere(i, carry):
            group_ref[i] = DEST
            return carry

        lax.fori_loop(0, GROUPS, nowhere, 0, unroll=16)
        zero = jnp.zeros((B, L), BF16)

        def wipe(i, carry):
            held[i] = zero
            return carry

        lax.fori_loop(0, 2 * GROUPS, wipe, 0, unroll=16)

    for g in range(ROWS_STEP):
        turned_p[g] = p_ref[g].astype(F32).T[:B].astype(BF16)

    low16 = low_lanes((ROWS_STEP, L))
    lane = lax.broadcasted_iota(jnp.int32, (B, L), 1)
    low = lane < B
    half = jnp.where(low, 0, 1)

    def insert(row, k, value, valid):
        e = (step * ROWS_STEP + row) * K + k
        d = dest_in[e]
        at = cursor[d]
        cursor[d] = at + valid
        at = jnp.where(valid == 1, at, POSITIONS)
        code_ref[at] = code_in[e]
        group_ref[at >> 2] = d
        tile = at >> 1
        held[tile] = jnp.where(half == (at & 1), value, held[tile].astype(F32)).astype(BF16)

    def pair_step(pair, carry):
        first = 2 * pair
        valid = jnp.where(first + 1 < K, 1, 0)
        second = jnp.minimum(first + 1, K - 1)
        for m in range(B // 2):
            one = a_ref[first, :, pl.ds(m * L, L)].astype(F32)
            two = a_ref[second, :, pl.ds(m * L, L)].astype(F32)
            wide[pl.ds(2 * m, ROWS_STEP, stride=PITCH), :] = jnp.where(
                low16, one, pltpu.roll(two, B, 1)
            )
            wide[pl.ds(2 * m + 1, ROWS_STEP, stride=PITCH), :] = jnp.where(
                low16, pltpu.roll(one, B, 1), two
            )
        for row in range(ROWS_STEP):
            block = wide[pl.ds(row * PITCH, B), :].astype(BF16)
            value = jnp.dot(turned_p[row], block, preferred_element_type=F32)
            turned = pltpu.roll(value, B, 1)
            insert(row, first, jnp.where(low, value, turned), 1)
            insert(row, second, jnp.where(low, turned, value), valid)
        return carry

    lax.fori_loop(0, (K + 1) // 2, pair_step, 0)

    @pl.when(step == pl.num_programs(0) - 1)
    def _():
        copy = pltpu.make_async_copy(held.at[pl.ds(0, 2 * GROUPS)], sorted_hbm, sem)
        copy.start()
        copy.wait()


def left(dest, code, a_turned, local):
    return pl.pallas_call(
        left_kernel,
        grid_spec=pltpu.PrefetchScalarGridSpec(
            num_scalar_prefetch=2,
            grid=(NB // ROWS_STEP,),
            in_specs=[
                pl.BlockSpec((K, ROWS_STEP, B * B), lambda i, *_: (0, i, 0)),
                pl.BlockSpec((ROWS_STEP, B, L), lambda i, *_: (i, 0, 0)),
            ],
            out_specs=[
                pl.BlockSpec(memory_space=pl.ANY),
                pl.BlockSpec(memory_space=pltpu.SMEM),
                pl.BlockSpec(memory_space=pltpu.SMEM),
                pl.BlockSpec(memory_space=pltpu.SMEM),
            ],
            scratch_shapes=[
                pltpu.VMEM((2 * GROUPS + 1, B, L), BF16),
                pltpu.VMEM((ROWS_STEP * PITCH, L), F32),
                pltpu.VMEM((ROWS_STEP, B, B), BF16),
                pltpu.SMEM((DEST,), jnp.int32),
                pltpu.SemaphoreType.DMA,
            ],
        ),
        out_shape=[
            jax.ShapeDtypeStruct((2 * GROUPS, B, L), BF16),
            jax.ShapeDtypeStruct((POSITIONS + GROUP,), jnp.int32),
            jax.ShapeDtypeStruct((GROUPS + 1,), jnp.int32),
            jax.ShapeDtypeStruct((1,), jnp.int32),
        ],
        compiler_params=params(56),
        cost_estimate=pl.CostEstimate(
            flops=2 * NB * K * B**3 * 16, bytes_accessed=60_000_000, transcendentals=0
        ),
        name="left",
    )(dest, code, a_turned, local)


def right_kernel(
    code_ref, group_ref, count_ref, bucket_ref, t_ref, local_hbm, ghost_hbm, out_ref,
    blocks, total, wide, halves, sems,
):
    step = pl.program_id(0)
    groups = count_ref[0]

    @pl.when(step == 0)
    def _():
        mine = pltpu.make_async_copy(local_hbm, blocks.at[pl.ds(0, LOCAL)], sems.at[0])
        others = pltpu.make_async_copy(
            ghost_hbm.at[:, pl.ds(0, SPAN), :],
            blocks.at[pl.ds(LOCAL, TILES)].reshape(PEERS, SPAN, L),
            sems.at[1],
        )
        mine.start()
        others.start()
        low = low_lanes((B, L))
        halves[0] = jnp.where(low, 1.0, 0.0).astype(BF16)
        halves[1] = jnp.where(low, 0.0, 1.0).astype(BF16)
        zero = jnp.zeros((B, L), F32)

        def clear(i, carry):
            total[i] = zero
            return carry

        lax.fori_loop(0, DEST + 1, clear, 0, unroll=8)
        mine.wait()
        others.wait()

    @pl.when(step < STEPS)
    def _():
        def batch(b, carry):
            for u in range(BATCH):
                here = b * BATCH + u
                group = step * CHUNK + here
                lhs = jnp.concatenate([t_ref[2 * here], t_ref[2 * here + 1]], axis=1)
                parts = []
                for w in range(GROUP):
                    code = code_ref[group * GROUP + w]
                    parts.append(blocks[code >> 1] * halves[code & 1])
                rhs = jnp.concatenate(parts, axis=0)
                d = group_ref[group]
                total[d] += jnp.dot(lhs, rhs, preferred_element_type=F32)
            return carry

        left_over = groups - step * CHUNK
        batches = jnp.clip((left_over + BATCH - 1) >> 4, 0, CHUNK // BATCH)
        lax.fori_loop(0, batches, batch, 0)

    @pl.when(step >= STEPS)
    def _():
        base = (step - STEPS) * S
        low = low_lanes((B // 2, L))

        def emit(part, carry):
            for u in range(9):
                s = part * 9 + u
                value = total[base + s]
                wide[pl.ds(u * B, B), :] = value + pltpu.roll(value, B, 1)
                even = wide[pl.ds(u * B, B // 2, stride=2), :]
                odd = wide[pl.ds(u * B + 1, B // 2, stride=2), :]
                out_ref[0, s] = jnp.where(low, even, odd).astype(BF16)
            return carry

        lax.fori_loop(0, S // 9, emit, 0)


def right(code, group, count, bucket, ordered, local, ghost, peers_y):
    last = STEPS - 1

    def t_map(i, code_ref, group_ref, count_ref, bucket_ref):
        used = jnp.maximum((count_ref[0] + CHUNK - 1) // CHUNK - 1, 0)
        return (jnp.minimum(jnp.minimum(i, last), used), 0, 0)

    def out_map(i, code_ref, group_ref, count_ref, bucket_ref):
        return (bucket_ref[jnp.maximum(i - STEPS, 0)], 0, 0, 0)

    return pl.pallas_call(
        right_kernel,
        grid_spec=pltpu.PrefetchScalarGridSpec(
            num_scalar_prefetch=4,
            grid=(STEPS + NCL,),
            in_specs=[
                pl.BlockSpec((2 * CHUNK, B, L), t_map),
                pl.BlockSpec(memory_space=pl.ANY),
                pl.BlockSpec(memory_space=pl.ANY),
            ],
            out_specs=pl.BlockSpec((1, S, B // 2, L), out_map),
            scratch_shapes=[
                pltpu.VMEM((LOCAL + TILES, B, L), BF16),
                pltpu.VMEM((DEST + 1, B, L), F32),
                pltpu.VMEM((9 * B, L), F32),
                pltpu.VMEM((2, B, L), BF16),
                pltpu.SemaphoreType.DMA((2,)),
            ],
        ),
        out_shape=jax.ShapeDtypeStruct((peers_y * CCAP, S, B // 2, L), BF16),
        compiler_params=params(48),
        name="right",
    )(code, group, count, bucket, ordered, local, ghost)


def place_kernel(from_ref, in_ref, out_ref, wide):
    step = pl.program_id(0)
    span = NCL * B // 2

    @pl.when(step < NCL)
    def _():
        for s in range(S):
            wide[pl.ds(s * span + step, B // 2, stride=NCL), :] = in_ref[0, s].astype(F32)

    @pl.when(step >= NCL)
    def _():
        def flatten(u, carry):
            start = pl.multiple_of(((step - NCL) * 9 + u) * span, span)
            for m in range(B // 2):
                out_ref[u, :, pl.ds(m * L, L)] = wide[
                    pl.ds(start + m * NCL, NCL), :
                ].astype(BF16)
            return carry

        lax.fori_loop(0, 9, flatten, 0)


def place(origin, arrived):
    return pl.pallas_call(
        place_kernel,
        grid_spec=pltpu.PrefetchScalarGridSpec(
            num_scalar_prefetch=1,
            grid=(NCL + S // 9,),
            in_specs=[
                pl.BlockSpec(
                    (1, S, B // 2, L), lambda i, o: (o[jnp.minimum(i, NCL - 1)], 0, 0, 0)
                )
            ],
            out_specs=pl.BlockSpec((9, NCL, B * B), lambda i, o: (jnp.maximum(i - NCL, 0), 0, 0)),
            scratch_shapes=[pltpu.VMEM((S * NCL * B // 2, L), F32)],
        ),
        out_shape=jax.ShapeDtypeStruct((S, NCL, B * B), BF16),
        compiler_params=params(32),
        name="place",
    )(origin, arrived)


def lists(a_source, agg_local, coarse_slot):
    dest = (agg_local[:, None] * S + coarse_slot).reshape(-1)
    ghost = a_source - NB + 2 * LOCAL
    code = jnp.where(a_source < NB, 2 * a_source, ghost).reshape(-1)
    return dest, code


def buckets(targets, peers_y):
    column = targets // NCL % peers_y
    order = jnp.arange(NCL)
    same = column[:, :, None] == column[:, None, :]
    earlier = order[None, None, :] < order[None, :, None]
    rank = jnp.sum((same & earlier).astype(jnp.int32), axis=2)
    return (column * CCAP + rank).astype(jnp.int32)


def origins(targets, me):
    peers_y = targets.shape[0]
    order = jnp.arange(NCL)
    rank = buckets(targets, peers_y) % CCAP
    source = jnp.arange(peers_y)[:, None] * CCAP + rank
    here = (targets // NCL % peers_y == me)[:, :, None]
    here = here & ((targets % NCL)[:, :, None] == order[None, None, :])
    return jnp.sum(jnp.where(here, source[:, :, None], 0), axis=(0, 1)).astype(jnp.int32)


def body(a_blocks, p_blocks, a_source, send_list, agg_local, coarse_slot, coarse_target):
    peers_y = lax.axis_size("py")
    me = lax.axis_index("py")
    modulus = peers_y * NCL
    note = jnp.zeros((NOTE, L), BF16).at[0, :NCL].set((coarse_target % modulus).astype(BF16))
    sending, local = pack(send_list.reshape(-1), p_blocks, note)
    ghost = lax.all_to_all(sending, ("px", "py"), split_axis=0, concat_axis=0, tiled=True)
    notes = lax.dynamic_slice(
        ghost, (lax.axis_index("px") * peers_y, SPAN, 0), (peers_y, 1, NCL)
    )
    origin = origins(notes.reshape(peers_y, NCL).astype(jnp.int32), me)
    bucket = buckets(coarse_target[None], peers_y)[0]
    dest, code = lists(a_source, agg_local, coarse_slot)
    ordered, code, group, count = left(dest, code, a_blocks.transpose(1, 0, 2), local)
    rows = right(code, group, count, bucket, ordered, local, ghost, peers_y)
    arrived = lax.all_to_all(
        rows.reshape(peers_y, CCAP * S * B // 2, L), "py", split_axis=0, concat_axis=0, tiled=True
    ).reshape(peers_y * CCAP, S, B // 2, L)
    return place(origin, arrived).transpose(1, 0, 2)


def solution(mesh):
    both = ("px", "py")
    in_specs = (
        P(both, None, None), P(both, None), P(both, None), P(both, None, None), P(both),
        P(both, None), P(both),
    )
    return jax.shard_map(
        body, mesh=mesh, in_specs=in_specs, out_specs=P(both, None, None), check_vma=False
    )
```

```python
import functools

import jax
import jax.numpy as jnp
from jax import lax
from jax.experimental import pallas as pl
from jax.experimental.pallas import tpu as pltpu
from jax.sharding import PartitionSpec as P

B = 64
L = 2 * B
NB = 96
K = 27
S = 27
AGG = 6
Q = 8
CCAP = 2
NCL = NB // AGG
PEERS = 128
DEST = NCL * S
PARTS = ((0, 9), (9, 18))
SIDE = 4
GROUP = 4
TILES = PEERS * Q // 2
LOCAL = NB + 2
GROUPS = 1024
POSITIONS = GROUPS * GROUP
CHUNK = 128
PITCH = 72
SPAN = Q // 2 * B
NOTE = 8
BATCH = 16
CHUNK_BITS = 7
BATCH_BITS = 4
STEPS = GROUPS // CHUNK
ROWS_STEP = 16
F32 = jnp.float32
BF16 = jnp.bfloat16


def low_lanes(shape):
    return lax.broadcasted_iota(jnp.int32, shape, 1) < B


def params(limit):
    return pltpu.CompilerParams(
        dimension_semantics=("arbitrary",), vmem_limit_bytes=limit * 1024 * 1024
    )


def pack_kernel(wanted, p_ref, note_ref, send_ref, local_ref, wide):
    step = pl.program_id(0)

    @pl.when(step == 0)
    def _():
        low = low_lanes((ROWS_STEP, L))

        def relayout(group, carry):
            row = pl.multiple_of(group * ROWS_STEP, ROWS_STEP)
            for m in range(B // 2):
                both = p_ref[pl.ds(row, ROWS_STEP), pl.ds(m * L, L)].astype(F32)
                turned = pltpu.roll(both, B, 1)
                even = jnp.where(low, both, turned)
                odd = jnp.where(low, turned, both)
                wide[pl.ds(2 * m, ROWS_STEP, stride=PITCH), :] = even
                wide[pl.ds(2 * m + 1, ROWS_STEP, stride=PITCH), :] = odd
            for g in range(ROWS_STEP):
                local_ref[row + g] = wide[pl.ds(g * PITCH, B), :].astype(BF16)
            return carry

        lax.fori_loop(0, NB // ROWS_STEP, relayout, 0)
        zero = jnp.zeros((B, L), BF16)
        local_ref[NB] = zero
        local_ref[NB + 1] = zero

    low = low_lanes((B, L))
    per_step = send_ref.shape[0]

    def fill(peer, carry):
        for u in range(Q // 2):
            slot = (step * per_step + peer) * Q + 2 * u
            first = wanted[slot]
            second = wanted[slot + 1]
            first = jnp.where(first < 0, NB, first)
            second = jnp.where(second < 0, NB, second)
            send_ref[peer, u * B : (u + 1) * B] = jnp.where(
                low, local_ref[first], local_ref[second]
            )
        send_ref[peer, SPAN:] = note_ref[...]
        return carry

    lax.fori_loop(0, per_step, fill, 0, unroll=2)


def pack(wanted, p_blocks, note):
    per_step = PEERS // 8
    return pl.pallas_call(
        pack_kernel,
        grid_spec=pltpu.PrefetchScalarGridSpec(
            num_scalar_prefetch=1,
            grid=(PEERS // per_step,),
            in_specs=[
                pl.BlockSpec((NB, B * B), lambda i, w: (0, 0)),
                pl.BlockSpec((NOTE, L), lambda i, w: (0, 0)),
            ],
            out_specs=[
                pl.BlockSpec((per_step, SPAN + NOTE, L), lambda i, w: (i, 0, 0)),
                pl.BlockSpec((LOCAL, B, L), lambda i, w: (0, 0, 0)),
            ],
            scratch_shapes=[pltpu.VMEM((ROWS_STEP * PITCH, L), F32)],
        ),
        out_shape=[
            jax.ShapeDtypeStruct((PEERS, SPAN + NOTE, L), BF16),
            jax.ShapeDtypeStruct((LOCAL, B, L), BF16),
        ],
        compiler_params=params(60),
        name="pack",
    )(wanted, p_blocks, note)


def left_kernel(
    dest_in, code_in, a_ref, p_ref, sorted_hbm, code_ref, group_ref, count_ref,
    held, wide, turned_p, cursor, sem,
):
    step = pl.program_id(0)

    @pl.when(step == 0)
    def _():
        def clear(d, carry):
            cursor[d] = 0
            return carry

        lax.fori_loop(0, DEST, clear, 0, unroll=8)

        def count(e, carry):
            d = dest_in[e]
            cursor[d] = cursor[d] + 1
            return carry

        lax.fori_loop(0, NB * K, count, 0, unroll=8)

        def place(d, at):
            here = cursor[d]
            cursor[d] = at
            return at + ((here + GROUP - 1) & -GROUP)

        at = 0
        for n, (start, width) in enumerate(PARTS):
            count_ref[2 * n] = at >> 2
            at = lax.fori_loop(start * NCL, (start + width) * NCL, place, at, unroll=8)
            count_ref[2 * n + 1] = at >> 2
            at = (at + GROUP * BATCH - 1) & -(GROUP * BATCH)

        def blank(i, carry):
            code_ref[i] = 2 * NB
            return carry

        lax.fori_loop(0, POSITIONS, blank, 0, unroll=16)

        def nowhere(i, carry):
            group_ref[i] = DEST
            return carry

        lax.fori_loop(0, GROUPS, nowhere, 0, unroll=16)
        zero = jnp.zeros((B, L), BF16)

        def wipe(i, carry):
            held[i] = zero
            return carry

        lax.fori_loop(0, 2 * GROUPS, wipe, 0, unroll=16)

    for g in range(ROWS_STEP):
        turned_p[g] = p_ref[g].astype(F32).T[:B].astype(BF16)

    low16 = low_lanes((ROWS_STEP, L))
    lane = lax.broadcasted_iota(jnp.int32, (B, L), 1)
    low = lane < B
    half = jnp.where(low, 0, 1)

    def insert(row, k, value, valid):
        e = (step * ROWS_STEP + row) * K + k
        d = dest_in[e]
        at = cursor[d]
        cursor[d] = at + valid
        at = jnp.where(valid == 1, at, POSITIONS)
        code_ref[at] = code_in[e]
        group_ref[at >> 2] = d
        tile = at >> 1
        held[tile] = jnp.where(half == (at & 1), value, held[tile].astype(F32)).astype(BF16)

    def pair_step(pair, carry):
        first = 2 * pair
        valid = jnp.where(first + 1 < K, 1, 0)
        second = jnp.minimum(first + 1, K - 1)
        for m in range(B // 2):
            one = a_ref[first, :, pl.ds(m * L, L)].astype(F32)
            two = a_ref[second, :, pl.ds(m * L, L)].astype(F32)
            wide[pl.ds(2 * m, ROWS_STEP, stride=PITCH), :] = jnp.where(
                low16, one, pltpu.roll(two, B, 1)
            )
            wide[pl.ds(2 * m + 1, ROWS_STEP, stride=PITCH), :] = jnp.where(
                low16, pltpu.roll(one, B, 1), two
            )
        for row in range(ROWS_STEP):
            block = wide[pl.ds(row * PITCH, B), :].astype(BF16)
            value = jnp.dot(turned_p[row], block, preferred_element_type=F32)
            turned = pltpu.roll(value, B, 1)
            insert(row, first, jnp.where(low, value, turned), 1)
            insert(row, second, jnp.where(low, turned, value), valid)
        return carry

    lax.fori_loop(0, (K + 1) // 2, pair_step, 0)

    @pl.when(step == pl.num_programs(0) - 1)
    def _():
        copy = pltpu.make_async_copy(held.at[pl.ds(0, 2 * GROUPS)], sorted_hbm, sem)
        copy.start()
        copy.wait()


def left(dest, code, a_turned, local):
    return pl.pallas_call(
        left_kernel,
        grid_spec=pltpu.PrefetchScalarGridSpec(
            num_scalar_prefetch=2,
            grid=(NB // ROWS_STEP,),
            in_specs=[
                pl.BlockSpec((K, ROWS_STEP, B * B), lambda i, *_: (0, i, 0)),
                pl.BlockSpec((ROWS_STEP, B, L), lambda i, *_: (i, 0, 0)),
            ],
            out_specs=[
                pl.BlockSpec(memory_space=pl.ANY),
                pl.BlockSpec(memory_space=pltpu.SMEM),
                pl.BlockSpec(memory_space=pltpu.SMEM),
                pl.BlockSpec(memory_space=pltpu.SMEM),
            ],
            scratch_shapes=[
                pltpu.VMEM((2 * GROUPS + 1, B, L), BF16),
                pltpu.VMEM((ROWS_STEP * PITCH, L), F32),
                pltpu.VMEM((ROWS_STEP, B, B), BF16),
                pltpu.SMEM((DEST,), jnp.int32),
                pltpu.SemaphoreType.DMA,
            ],
        ),
        out_shape=[
            jax.ShapeDtypeStruct((2 * GROUPS, B, L), BF16),
            jax.ShapeDtypeStruct((POSITIONS + GROUP,), jnp.int32),
            jax.ShapeDtypeStruct((GROUPS + 1,), jnp.int32),
            jax.ShapeDtypeStruct((2 * len(PARTS),), jnp.int32),
        ],
        compiler_params=params(56),
        cost_estimate=pl.CostEstimate(
            flops=2 * NB * K * B**3 * 16, bytes_accessed=60_000_000, transcendentals=0
        ),
        name="left",
    )(dest, code, a_turned, local)


def right_kernel(
    part, code_ref, group_ref, count_ref, bucket_ref, t_ref, local_hbm, ghost_hbm, out_hbm,
    blocks, total, wide, staged, halves, sems, out_sems,
):
    step = pl.program_id(0)
    start, width = PARTS[part]
    first = count_ref[2 * part]
    last = count_ref[2 * part + 1]
    origin = (first >> CHUNK_BITS) << CHUNK_BITS

    @pl.when(step == 0)
    def _():
        mine = pltpu.make_async_copy(local_hbm, blocks.at[pl.ds(0, LOCAL)], sems.at[0])
        others = pltpu.make_async_copy(
            ghost_hbm.at[:, pl.ds(0, SPAN), :],
            blocks.at[pl.ds(LOCAL, TILES)].reshape(PEERS, SPAN, L),
            sems.at[1],
        )
        mine.start()
        others.start()
        low = low_lanes((16, L))
        halves[0] = jnp.where(low, 1.0, 0.0).astype(BF16)
        halves[1] = jnp.where(low, 0.0, 1.0).astype(BF16)
        zero = jnp.zeros((B, L), F32)

        def clear(i, carry):
            total[i] = zero
            return carry

        lax.fori_loop(0, width * NCL + 1, clear, 0, unroll=8)
        mine.wait()
        others.wait()

    def batch(b, carry):
        for u in range(BATCH):
            here = b * BATCH + u
            group = origin + step * CHUNK + here
            lhs = jnp.concatenate([t_ref[2 * here], t_ref[2 * here + 1]], axis=1)
            parts = []
            for w in range(GROUP):
                code = code_ref[group * GROUP + w]
                block = blocks[code >> 1].reshape(B // 16, 16, L)
                parts.append((block * halves[code & 1][None]).reshape(B, L))
            rhs = jnp.concatenate(parts, axis=0)
            d = jnp.minimum(group_ref[group] - start * NCL, width * NCL)
            total[d] += jnp.dot(lhs, rhs, preferred_element_type=F32)
        return carry

    at = origin + step * CHUNK
    begin = jnp.clip((first - at) >> BATCH_BITS, 0, CHUNK // BATCH)
    end = jnp.clip((last - at + BATCH - 1) >> BATCH_BITS, 0, CHUNK // BATCH)
    lax.fori_loop(begin, end, batch, 0)

    @pl.when(step == STEPS - 1)
    def _():
        low = low_lanes((B // 2, L))
        copies = [
            pltpu.make_async_copy(staged.at[c], out_hbm.at[bucket_ref[c]], out_sems.at[c])
            for c in range(NCL)
        ]
        for c in range(NCL):

            def emit(s, carry, c=c):
                value = total[s * NCL + c]
                row = pl.multiple_of(s * B, B)
                wide[pl.ds(row, B), :] = value + pltpu.roll(value, B, 1)
                even = wide[pl.ds(row, B // 2, stride=2), :]
                odd = wide[pl.ds(row + 1, B // 2, stride=2), :]
                staged[c, s] = jnp.where(low, even, odd).astype(BF16)
                return carry

            lax.fori_loop(0, width, emit, 0, unroll=True)
            copies[c].start()
        for copy in copies:
            copy.wait()


def right(part, code, group, count, bucket, ordered, local, ghost, peers_y):
    width = PARTS[part][1]

    def t_map(i, code_ref, group_ref, count_ref, bucket_ref):
        block = (count_ref[2 * part] >> CHUNK_BITS) + i
        used = jnp.maximum(count_ref[2 * part + 1] - 1, 0) >> CHUNK_BITS
        return (jnp.minimum(block, used), 0, 0)

    return pl.pallas_call(
        functools.partial(right_kernel, part),
        grid_spec=pltpu.PrefetchScalarGridSpec(
            num_scalar_prefetch=4,
            grid=(STEPS,),
            in_specs=[
                pl.BlockSpec((2 * CHUNK, B, L), t_map),
                pl.BlockSpec(memory_space=pl.ANY),
                pl.BlockSpec(memory_space=pl.ANY),
            ],
            out_specs=pl.BlockSpec(memory_space=pl.ANY),
            scratch_shapes=[
                pltpu.VMEM((LOCAL + TILES, B, L), BF16),
                pltpu.VMEM((width * NCL + 1, B, L), F32),
                pltpu.VMEM((width * B, L), F32),
                pltpu.VMEM((NCL, width, B // 2, L), BF16),
                pltpu.VMEM((2, 16, L), BF16),
                pltpu.SemaphoreType.DMA((2,)),
                pltpu.SemaphoreType.DMA((NCL,)),
            ],
        ),
        out_shape=jax.ShapeDtypeStruct((peers_y * CCAP, width, B // 2, L), BF16),
        compiler_params=params(60),
        cost_estimate=pl.CostEstimate(
            flops=NB * K * B**3 * 32, bytes_accessed=30_000_000, transcendentals=0
        ),
        name="right%d" % part,
    )(code, group, count, bucket, ordered, local, ghost)


def exchange_kernel(x_ref, out_ref, send_sems, recv_sems, own_sem):
    px, me = lax.axis_index("px"), lax.axis_index("py")
    shifts = sorted(
        ((dx, dy) for dx in range(SIDE) for dy in range(SIDE) if dx or dy),
        key=lambda o: -min(o[0], SIDE - o[0]) - min(o[1], SIDE - o[1]),
    )

    def peer(shift):
        return (me // SIDE + shift[0]) % SIDE * SIDE + (me + shift[1]) % SIDE

    barrier = pltpu.get_barrier_semaphore()
    for shift in shifts:
        pl.semaphore_signal(
            barrier, inc=1, device_id=(px, peer(shift)), device_id_type=pl.DeviceIdType.MESH
        )
    pl.semaphore_wait(barrier, len(shifts))
    copies = []
    for n, shift in enumerate(shifts):
        copy = pltpu.make_async_remote_copy(
            src_ref=x_ref.at[peer(shift)],
            dst_ref=out_ref.at[me],
            send_sem=send_sems.at[n],
            recv_sem=recv_sems.at[n],
            device_id=(px, peer(shift)),
            device_id_type=pl.DeviceIdType.MESH,
        )
        copy.start()
        copies.append(copy)
    own = pltpu.make_async_copy(x_ref.at[me], out_ref.at[me], own_sem)
    own.start()
    own.wait()
    for copy in copies:
        copy.wait()


def exchange(rows):
    peers = SIDE * SIDE
    return pl.pallas_call(
        exchange_kernel,
        in_specs=[pl.BlockSpec(memory_space=pl.ANY)],
        out_specs=pl.BlockSpec(memory_space=pl.ANY),
        out_shape=jax.ShapeDtypeStruct(rows.shape, rows.dtype),
        scratch_shapes=[
            pltpu.SemaphoreType.DMA((peers - 1,)),
            pltpu.SemaphoreType.DMA((peers - 1,)),
            pltpu.SemaphoreType.DMA,
        ],
        compiler_params=pltpu.CompilerParams(
            collective_id=0, has_side_effects=True, vmem_limit_bytes=60 * 1024 * 1024
        ),
        cost_estimate=pl.CostEstimate(
            flops=0, bytes_accessed=300_000_000, transcendentals=0
        ),
        name="exchange",
    )(rows)


AHEAD = 4


def place_kernel(from_ref, *refs):
    ins, out_ref, wide = refs[:-2], refs[-2], refs[-1]
    step = pl.program_id(0)
    span = NCL * B // 2

    @pl.when(step < NCL // AHEAD)
    def _():
        for n, (start, width) in enumerate(PARTS):
            for j in range(AHEAD):
                rows = ins[n * AHEAD + j]

                def spread(s, carry, start=start, rows=rows, j=j):
                    at = (start + s) * span + step * AHEAD + j
                    wide[pl.ds(at, B // 2, stride=NCL), :] = rows[0, s].astype(F32)
                    return carry

                lax.fori_loop(0, width, spread, 0, unroll=True)

    @pl.when(step >= NCL // AHEAD)
    def _():
        def flatten(u, carry):
            start = pl.multiple_of(((step - NCL // AHEAD) * 9 + u) * span, span)
            for m in range(B // 2):
                out_ref[u, :, pl.ds(m * L, L)] = wide[
                    pl.ds(start + m * NCL, NCL), :
                ].astype(BF16)
            return carry

        lax.fori_loop(0, 9, flatten, 0)


def place(origin, arrived):
    turns = NCL // AHEAD

    def spec(width, j):
        return pl.BlockSpec(
            (1, width, B // 2, L),
            lambda i, o: (o[jnp.minimum(i, turns - 1) * AHEAD + j], 0, 0, 0),
        )

    return pl.pallas_call(
        place_kernel,
        grid_spec=pltpu.PrefetchScalarGridSpec(
            num_scalar_prefetch=1,
            grid=(turns + S // 9,),
            in_specs=[spec(width, j) for _, width in PARTS for j in range(AHEAD)],
            out_specs=pl.BlockSpec(
                (9, NCL, B * B), lambda i, o: (jnp.maximum(i - turns, 0), 0, 0)
            ),
            scratch_shapes=[pltpu.VMEM((S * NCL * B // 2, L), F32)],
        ),
        out_shape=jax.ShapeDtypeStruct((S, NCL, B * B), BF16),
        compiler_params=params(60),
        name="place",
    )(origin, *[rows for rows in arrived for _ in range(AHEAD)])


def lists(a_source, agg_local, coarse_slot):
    dest = (coarse_slot * NCL + agg_local[:, None]).reshape(-1)
    ghost = a_source - NB + 2 * LOCAL
    code = jnp.where(a_source < NB, 2 * a_source, ghost).reshape(-1)
    return dest, code


def buckets(targets, peers_y):
    column = targets // NCL % peers_y
    order = jnp.arange(NCL)
    same = column[:, :, None] == column[:, None, :]
    earlier = order[None, None, :] < order[None, :, None]
    rank = jnp.sum((same & earlier).astype(jnp.int32), axis=2)
    return (column * CCAP + rank).astype(jnp.int32)


def origins(targets, me):
    peers_y = targets.shape[0]
    order = jnp.arange(NCL)
    rank = buckets(targets, peers_y) % CCAP
    source = jnp.arange(peers_y)[:, None] * CCAP + rank
    here = (targets // NCL % peers_y == me)[:, :, None]
    here = here & ((targets % NCL)[:, :, None] == order[None, None, :])
    return jnp.sum(jnp.where(here, source[:, :, None], 0), axis=(0, 1)).astype(jnp.int32)


def body(a_blocks, p_blocks, a_source, send_list, agg_local, coarse_slot, coarse_target):
    peers_y = lax.axis_size("py")
    me = lax.axis_index("py")
    modulus = peers_y * NCL
    note = jnp.zeros((NOTE, L), BF16).at[0, :NCL].set((coarse_target % modulus).astype(BF16))
    sending, local = pack(send_list.reshape(-1), p_blocks, note)
    ghost = lax.all_to_all(sending, ("px", "py"), split_axis=0, concat_axis=0, tiled=True)
    notes = lax.dynamic_slice(
        ghost, (lax.axis_index("px") * peers_y, SPAN, 0), (peers_y, 1, NCL)
    )
    origin = origins(notes.reshape(peers_y, NCL).astype(jnp.int32), me)
    bucket = buckets(coarse_target[None], peers_y)[0]
    dest, code = lists(a_source, agg_local, coarse_slot)
    ordered, code, group, count = left(dest, code, a_blocks.transpose(1, 0, 2), local)
    arrived = []
    for part, (_, width) in enumerate(PARTS):
        rows = right(part, code, group, count, bucket, ordered, local, ghost, peers_y)
        rows = rows.reshape(peers_y, CCAP * width * B // 2, L)
        if part == 0:
            rows = lax.all_to_all(rows, "py", split_axis=0, concat_axis=0, tiled=True)
        else:
            rows = exchange(rows)
        arrived.append(rows.reshape(peers_y * CCAP, width, B // 2, L))
    return place(origin, arrived).transpose(1, 0, 2)


def solution(mesh):
    both = ("px", "py")
    in_specs = (
        P(both, None, None), P(both, None), P(both, None), P(both, None, None), P(both),
        P(both, None), P(both),
    )
    return jax.shard_map(
        body, mesh=mesh, in_specs=in_specs, out_specs=P(both, None, None), check_vma=False
    )
```

```python
import functools

import jax
import jax.numpy as jnp
from jax import lax
from jax.experimental import pallas as pl
from jax.experimental.pallas import tpu as pltpu
from jax.sharding import PartitionSpec as P

B = 64
L = 2 * B
NB = 96
K = 27
S = 27
AGG = 6
Q = 8
CCAP = 2
NCL = NB // AGG
PEERS = 128
DEST = NCL * S
PARTS = ((0, 9), (9, 18))
SIDE = 4
GROUP = 4
TILES = PEERS * Q // 2
LOCAL = NB + 2
GROUPS = 1024
POSITIONS = GROUPS * GROUP
CHUNK = 128
PITCH = 72
SPAN = Q // 2 * B
NOTE = 8
BATCH = 16
CHUNK_BITS = 7
BATCH_BITS = 4
STEPS = GROUPS // CHUNK
ROWS_STEP = 16
F32 = jnp.float32
BF16 = jnp.bfloat16


def low_lanes(shape):
    return lax.broadcasted_iota(jnp.int32, shape, 1) < B


def params(limit):
    return pltpu.CompilerParams(
        dimension_semantics=("arbitrary",), vmem_limit_bytes=limit * 1024 * 1024
    )


def pack_kernel(wanted, p_ref, send_ref, local_ref, wide):
    step = pl.program_id(0)

    @pl.when(step == 0)
    def _():
        low = low_lanes((ROWS_STEP, L))

        def relayout(group, carry):
            row = pl.multiple_of(group * ROWS_STEP, ROWS_STEP)
            for m in range(B // 2):
                both = p_ref[pl.ds(row, ROWS_STEP), pl.ds(m * L, L)].astype(F32)
                turned = pltpu.roll(both, B, 1)
                even = jnp.where(low, both, turned)
                odd = jnp.where(low, turned, both)
                wide[pl.ds(2 * m, ROWS_STEP, stride=PITCH), :] = even
                wide[pl.ds(2 * m + 1, ROWS_STEP, stride=PITCH), :] = odd
            for g in range(ROWS_STEP):
                local_ref[row + g] = wide[pl.ds(g * PITCH, B), :].astype(BF16)
            return carry

        lax.fori_loop(0, NB // ROWS_STEP, relayout, 0)
        zero = jnp.zeros((B, L), BF16)
        local_ref[NB] = zero
        local_ref[NB + 1] = zero

    low = low_lanes((B, L))
    per_step = send_ref.shape[0]

    def fill(peer, carry):
        for u in range(Q // 2):
            first = wanted[2 * u, step * per_step + peer]
            second = wanted[2 * u + 1, step * per_step + peer]
            first = jnp.where(first < 0, NB, first)
            second = jnp.where(second < 0, NB, second)
            send_ref[peer, u * B : (u + 1) * B] = jnp.where(
                low, local_ref[first], local_ref[second]
            )
        return carry

    lax.fori_loop(0, per_step, fill, 0, unroll=2)


def pack(wanted, p_blocks):
    per_step = PEERS // 8
    return pl.pallas_call(
        pack_kernel,
        grid_spec=pltpu.PrefetchScalarGridSpec(
            num_scalar_prefetch=1,
            grid=(PEERS // per_step,),
            in_specs=[
                pl.BlockSpec((NB, B * B), lambda i, w: (0, 0)),
            ],
            out_specs=[
                pl.BlockSpec((per_step, SPAN, L), lambda i, w: (i, 0, 0)),
                pl.BlockSpec((LOCAL, B, L), lambda i, w: (0, 0, 0)),
            ],
            scratch_shapes=[pltpu.VMEM((ROWS_STEP * PITCH, L), F32)],
        ),
        out_shape=[
            jax.ShapeDtypeStruct((PEERS, SPAN, L), BF16),
            jax.ShapeDtypeStruct((LOCAL, B, L), BF16),
        ],
        compiler_params=params(60),
        name="pack",
    )(wanted, p_blocks)


def left_kernel(
    dest_in, code_in, a_ref, p_ref, sorted_hbm, code_ref, group_ref, count_ref,
    held, wide, turned_p, cursor, sem,
):
    step = pl.program_id(0)

    @pl.when(step == 0)
    def _():
        def clear(d, carry):
            cursor[d] = 0
            return carry

        lax.fori_loop(0, DEST, clear, 0, unroll=8)

        def count(e, carry):
            d = dest_in[e]
            cursor[d] = cursor[d] + 1
            return carry

        lax.fori_loop(0, NB * K, count, 0, unroll=8)

        def place(d, at):
            here = cursor[d]
            cursor[d] = at
            return at + ((here + GROUP - 1) & -GROUP)

        at = 0
        for n, (start, width) in enumerate(PARTS):
            count_ref[2 * n] = at >> 2
            at = lax.fori_loop(start * NCL, (start + width) * NCL, place, at, unroll=8)
            count_ref[2 * n + 1] = at >> 2
            at = (at + GROUP * BATCH - 1) & -(GROUP * BATCH)

        def blank(i, carry):
            code_ref[i] = 2 * NB
            return carry

        lax.fori_loop(0, POSITIONS, blank, 0, unroll=16)

        def nowhere(i, carry):
            group_ref[i] = DEST
            return carry

        lax.fori_loop(0, GROUPS, nowhere, 0, unroll=16)
        zero = jnp.zeros((B, L), BF16)

        def wipe(i, carry):
            held[i] = zero
            return carry

        lax.fori_loop(0, 2 * GROUPS, wipe, 0, unroll=16)

    for g in range(ROWS_STEP):
        turned_p[g] = p_ref[g].astype(F32).T[:B].astype(BF16)

    low16 = low_lanes((ROWS_STEP, L))
    lane = lax.broadcasted_iota(jnp.int32, (B, L), 1)
    low = lane < B
    half = jnp.where(low, 0, 1)

    def insert(row, k, value, valid):
        e = (step * ROWS_STEP + row) * K + k
        d = dest_in[e]
        at = cursor[d]
        cursor[d] = at + valid
        at = jnp.where(valid == 1, at, POSITIONS)
        code_ref[at] = code_in[e]
        group_ref[at >> 2] = d
        tile = at >> 1
        held[tile] = jnp.where(half == (at & 1), value, held[tile].astype(F32)).astype(BF16)

    def pair_step(pair, carry):
        first = 2 * pair
        valid = jnp.where(first + 1 < K, 1, 0)
        second = jnp.minimum(first + 1, K - 1)
        for m in range(B // 2):
            one = a_ref[first, :, pl.ds(m * L, L)].astype(F32)
            two = a_ref[second, :, pl.ds(m * L, L)].astype(F32)
            wide[pl.ds(2 * m, ROWS_STEP, stride=PITCH), :] = jnp.where(
                low16, one, pltpu.roll(two, B, 1)
            )
            wide[pl.ds(2 * m + 1, ROWS_STEP, stride=PITCH), :] = jnp.where(
                low16, pltpu.roll(one, B, 1), two
            )
        for row in range(ROWS_STEP):
            block = wide[pl.ds(row * PITCH, B), :].astype(BF16)
            value = jnp.dot(turned_p[row], block, preferred_element_type=F32)
            turned = pltpu.roll(value, B, 1)
            insert(row, first, jnp.where(low, value, turned), 1)
            insert(row, second, jnp.where(low, turned, value), valid)
        return carry

    lax.fori_loop(0, (K + 1) // 2, pair_step, 0)

    @pl.when(step == pl.num_programs(0) - 1)
    def _():
        copy = pltpu.make_async_copy(held.at[pl.ds(0, 2 * GROUPS)], sorted_hbm, sem)
        copy.start()
        copy.wait()


def left(dest, code, a_turned, local):
    return pl.pallas_call(
        left_kernel,
        grid_spec=pltpu.PrefetchScalarGridSpec(
            num_scalar_prefetch=2,
            grid=(NB // ROWS_STEP,),
            in_specs=[
                pl.BlockSpec((K, ROWS_STEP, B * B), lambda i, *_: (0, i, 0)),
                pl.BlockSpec((ROWS_STEP, B, L), lambda i, *_: (i, 0, 0)),
            ],
            out_specs=[
                pl.BlockSpec(memory_space=pl.ANY),
                pl.BlockSpec(memory_space=pltpu.SMEM),
                pl.BlockSpec(memory_space=pltpu.SMEM),
                pl.BlockSpec(memory_space=pltpu.SMEM),
            ],
            scratch_shapes=[
                pltpu.VMEM((2 * GROUPS + 1, B, L), BF16),
                pltpu.VMEM((ROWS_STEP * PITCH, L), F32),
                pltpu.VMEM((ROWS_STEP, B, B), BF16),
                pltpu.SMEM((DEST,), jnp.int32),
                pltpu.SemaphoreType.DMA,
            ],
        ),
        out_shape=[
            jax.ShapeDtypeStruct((2 * GROUPS, B, L), BF16),
            jax.ShapeDtypeStruct((POSITIONS + GROUP,), jnp.int32),
            jax.ShapeDtypeStruct((GROUPS + 1,), jnp.int32),
            jax.ShapeDtypeStruct((2 * len(PARTS),), jnp.int32),
        ],
        compiler_params=params(56),
        cost_estimate=pl.CostEstimate(
            flops=2 * NB * K * B**3 * 16, bytes_accessed=60_000_000, transcendentals=0
        ),
        name="left",
    )(dest, code, a_turned, local)


def right_kernel(
    part, code_ref, group_ref, count_ref, bucket_ref, t_ref, local_hbm, ghost_hbm, out_hbm,
    blocks, total, wide, staged, halves, sems, out_sems,
):
    step = pl.program_id(0)
    start, width = PARTS[part]
    first = count_ref[2 * part]
    last = count_ref[2 * part + 1]
    origin = (first >> CHUNK_BITS) << CHUNK_BITS

    @pl.when(step == 0)
    def _():
        mine = pltpu.make_async_copy(local_hbm, blocks.at[pl.ds(0, LOCAL)], sems.at[0])
        others = pltpu.make_async_copy(
            ghost_hbm,
            blocks.at[pl.ds(LOCAL, TILES)].reshape(PEERS, SPAN, L),
            sems.at[1],
        )
        mine.start()
        others.start()
        low = low_lanes((16, L))
        halves[0] = jnp.where(low, 1.0, 0.0).astype(BF16)
        halves[1] = jnp.where(low, 0.0, 1.0).astype(BF16)
        zero = jnp.zeros((B, L), F32)

        def clear(i, carry):
            total[i] = zero
            return carry

        lax.fori_loop(0, width * NCL + 1, clear, 0, unroll=8)
        mine.wait()
        others.wait()

    def batch(b, carry):
        for u in range(BATCH):
            here = b * BATCH + u
            group = origin + step * CHUNK + here
            lhs = jnp.concatenate([t_ref[2 * here], t_ref[2 * here + 1]], axis=1)
            parts = []
            for w in range(GROUP):
                code = code_ref[group * GROUP + w]
                block = blocks[code >> 1].reshape(B // 16, 16, L)
                parts.append((block * halves[code & 1][None]).reshape(B, L))
            rhs = jnp.concatenate(parts, axis=0)
            d = jnp.minimum(group_ref[group] - start * NCL, width * NCL)
            total[d] += jnp.dot(lhs, rhs, preferred_element_type=F32)
        return carry

    at = origin + step * CHUNK
    begin = jnp.clip((first - at) >> BATCH_BITS, 0, CHUNK // BATCH)
    end = jnp.clip((last - at + BATCH - 1) >> BATCH_BITS, 0, CHUNK // BATCH)
    lax.fori_loop(begin, end, batch, 0)

    @pl.when(step == STEPS - 1)
    def _():
        low = low_lanes((B // 2, L))
        copies = [
            pltpu.make_async_copy(staged.at[c], out_hbm.at[bucket_ref[c]], out_sems.at[c])
            for c in range(NCL)
        ]
        for c in range(NCL):

            def emit(s, carry, c=c):
                value = total[s * NCL + c]
                row = pl.multiple_of(s * B, B)
                wide[pl.ds(row, B), :] = value + pltpu.roll(value, B, 1)
                even = wide[pl.ds(row, B // 2, stride=2), :]
                odd = wide[pl.ds(row + 1, B // 2, stride=2), :]
                staged[c, s] = jnp.where(low, even, odd).astype(BF16)
                return carry

            lax.fori_loop(0, width, emit, 0, unroll=True)
            copies[c].start()
        for copy in copies:
            copy.wait()


def right(part, code, group, count, bucket, ordered, local, ghost, peers_y):
    width = PARTS[part][1]

    def t_map(i, code_ref, group_ref, count_ref, bucket_ref):
        block = (count_ref[2 * part] >> CHUNK_BITS) + i
        used = jnp.maximum(count_ref[2 * part + 1] - 1, 0) >> CHUNK_BITS
        return (jnp.minimum(block, used), 0, 0)

    return pl.pallas_call(
        functools.partial(right_kernel, part),
        grid_spec=pltpu.PrefetchScalarGridSpec(
            num_scalar_prefetch=4,
            grid=(STEPS,),
            in_specs=[
                pl.BlockSpec((2 * CHUNK, B, L), t_map),
                pl.BlockSpec(memory_space=pl.ANY),
                pl.BlockSpec(memory_space=pl.ANY),
            ],
            out_specs=pl.BlockSpec(memory_space=pl.ANY),
            scratch_shapes=[
                pltpu.VMEM((LOCAL + TILES, B, L), BF16),
                pltpu.VMEM((width * NCL + 1, B, L), F32),
                pltpu.VMEM((width * B, L), F32),
                pltpu.VMEM((NCL, width, B // 2, L), BF16),
                pltpu.VMEM((2, 16, L), BF16),
                pltpu.SemaphoreType.DMA((2,)),
                pltpu.SemaphoreType.DMA((NCL,)),
            ],
        ),
        out_shape=jax.ShapeDtypeStruct((peers_y * CCAP, width, B // 2, L), BF16),
        compiler_params=params(63),
        cost_estimate=pl.CostEstimate(
            flops=NB * K * B**3 * 32, bytes_accessed=30_000_000, transcendentals=0
        ),
        name="right%d" % part,
    )(code, group, count, bucket, ordered, local, ghost)


def exchange_kernel(x_ref, out_ref, send_sems, recv_sems, own_sem):
    px, me = lax.axis_index("px"), lax.axis_index("py")
    shifts = sorted(
        ((dx, dy) for dx in range(SIDE) for dy in range(SIDE) if dx or dy),
        key=lambda o: -min(o[0], SIDE - o[0]) - min(o[1], SIDE - o[1]),
    )

    def peer(shift):
        return (me // SIDE + shift[0]) % SIDE * SIDE + (me + shift[1]) % SIDE

    barrier = pltpu.get_barrier_semaphore()
    for shift in shifts:
        pl.semaphore_signal(
            barrier, inc=1, device_id=(px, peer(shift)), device_id_type=pl.DeviceIdType.MESH
        )
    pl.semaphore_wait(barrier, len(shifts))
    copies = []
    for n, shift in enumerate(shifts):
        copy = pltpu.make_async_remote_copy(
            src_ref=x_ref.at[peer(shift)],
            dst_ref=out_ref.at[me],
            send_sem=send_sems.at[n],
            recv_sem=recv_sems.at[n],
            device_id=(px, peer(shift)),
            device_id_type=pl.DeviceIdType.MESH,
        )
        copy.start()
        copies.append(copy)
    own = pltpu.make_async_copy(x_ref.at[me], out_ref.at[me], own_sem)
    own.start()
    own.wait()
    for copy in copies:
        copy.wait()


def exchange(rows, collective_id, name):
    peers = SIDE * SIDE
    return pl.pallas_call(
        exchange_kernel,
        in_specs=[pl.BlockSpec(memory_space=pl.ANY)],
        out_specs=pl.BlockSpec(memory_space=pl.ANY),
        out_shape=jax.ShapeDtypeStruct(rows.shape, rows.dtype),
        scratch_shapes=[
            pltpu.SemaphoreType.DMA((peers - 1,)),
            pltpu.SemaphoreType.DMA((peers - 1,)),
            pltpu.SemaphoreType.DMA,
        ],
        compiler_params=pltpu.CompilerParams(
            collective_id=collective_id, has_side_effects=True, vmem_limit_bytes=63 * 1024 * 1024
        ),
        cost_estimate=pl.CostEstimate(
            flops=0, bytes_accessed=300_000_000, transcendentals=0
        ),
        name=name,
    )(rows)


AHEAD = 4


def place_kernel(from_ref, *refs):
    ins, out_ref, wide = refs[:-2], refs[-2], refs[-1]
    step = pl.program_id(0)
    span = NCL * B // 2

    @pl.when(step < NCL // AHEAD)
    def _():
        for n, (start, width) in enumerate(PARTS):
            for j in range(AHEAD):
                rows = ins[n * AHEAD + j]

                def spread(s, carry, start=start, rows=rows, j=j):
                    at = (start + s) * span + step * AHEAD + j
                    wide[pl.ds(at, B // 2, stride=NCL), :] = rows[0, s].astype(F32)
                    return carry

                lax.fori_loop(0, width, spread, 0, unroll=True)

    @pl.when(step >= NCL // AHEAD)
    def _():
        def flatten(u, carry):
            start = pl.multiple_of(((step - NCL // AHEAD) * 9 + u) * span, span)
            for m in range(B // 2):
                out_ref[u, :, pl.ds(m * L, L)] = wide[
                    pl.ds(start + m * NCL, NCL), :
                ].astype(BF16)
            return carry

        lax.fori_loop(0, 9, flatten, 0)


def place(origin, arrived):
    turns = NCL // AHEAD

    def spec(width, j):
        return pl.BlockSpec(
            (1, width, B // 2, L),
            lambda i, o: (o[jnp.minimum(i, turns - 1) * AHEAD + j], 0, 0, 0),
        )

    return pl.pallas_call(
        place_kernel,
        grid_spec=pltpu.PrefetchScalarGridSpec(
            num_scalar_prefetch=1,
            grid=(turns + S // 9,),
            in_specs=[spec(width, j) for _, width in PARTS for j in range(AHEAD)],
            out_specs=pl.BlockSpec(
                (9, NCL, B * B), lambda i, o: (jnp.maximum(i - turns, 0), 0, 0)
            ),
            scratch_shapes=[pltpu.VMEM((S * NCL * B // 2, L), F32)],
        ),
        out_shape=jax.ShapeDtypeStruct((S, NCL, B * B), BF16),
        compiler_params=params(60),
        name="place",
    )(origin, *[rows for rows in arrived for _ in range(AHEAD)])


def lists(a_source, agg_local, coarse_slot):
    dest = (coarse_slot * NCL + agg_local[:, None]).reshape(-1)
    ghost = a_source - NB + 2 * LOCAL
    code = jnp.where(a_source < NB, 2 * a_source, ghost).reshape(-1)
    return dest, code


def buckets(targets, peers_y):
    column = targets // NCL % peers_y
    order = jnp.arange(NCL)
    same = column[:, :, None] == column[:, None, :]
    earlier = order[None, None, :] < order[None, :, None]
    rank = jnp.sum((same & earlier).astype(jnp.int32), axis=2)
    return (column * CCAP + rank).astype(jnp.int32)


def origins(targets, me):
    peers_y = targets.shape[0]
    order = jnp.arange(NCL)
    rank = buckets(targets, peers_y) % CCAP
    source = jnp.arange(peers_y)[:, None] * CCAP + rank
    here = (targets // NCL % peers_y == me)[:, :, None]
    here = here & ((targets % NCL)[:, :, None] == order[None, None, :])
    return jnp.sum(jnp.where(here, source[:, :, None], 0), axis=(0, 1)).astype(jnp.int32)


def body(a_blocks, p_blocks, a_source, send_list, agg_local, coarse_slot, coarse_target):
    peers_y = lax.axis_size("py")
    me = lax.axis_index("py")
    sending, local = pack(send_list.reshape(PEERS, Q).T, p_blocks)
    ghost = lax.all_to_all(sending, ("px", "py"), split_axis=0, concat_axis=0, tiled=True)
    bucket = buckets(coarse_target[None], peers_y)[0]
    dest, code = lists(a_source, agg_local, coarse_slot)
    ordered, code, group, count = left(dest, code, a_blocks.transpose(1, 0, 2), local)
    tied, _ = lax.optimization_barrier((coarse_target, count))
    note = jnp.broadcast_to(jnp.pad(tied, (0, L - NCL)), (peers_y, NOTE, L))
    targets = exchange(note, 1, "targets")[:, 0, :NCL]
    origin = origins(targets, me)
    bucket = jnp.concatenate([bucket, origin])
    arrived = []
    for part, (_, width) in enumerate(PARTS):
        rows = right(part, code, group, count, bucket, ordered, local, ghost, peers_y)
        rows = rows.reshape(peers_y, CCAP * width * B // 2, L)
        if part == 0:
            rows = lax.all_to_all(rows, "py", split_axis=0, concat_axis=0, tiled=True)
        else:
            rows = exchange(rows, 0, "exchange")
        arrived.append(rows.reshape(peers_y * CCAP, width, B // 2, L))
    return place(origin, arrived).transpose(1, 0, 2)


def solution(mesh):
    both = ("px", "py")
    in_specs = (
        P(both, None, None), P(both, None), P(both, None), P(both, None, None), P(both),
        P(both, None), P(both),
    )
    return jax.shard_map(
        body, mesh=mesh, in_specs=in_specs, out_specs=P(both, None, None), check_vma=False
    )
```

```python
import functools

import jax
import jax.numpy as jnp
from jax import lax
from jax.experimental import pallas as pl
from jax.experimental.pallas import tpu as pltpu
from jax.sharding import PartitionSpec as P

B = 64
L = 2 * B
NB = 96
K = 27
S = 27
AGG = 6
Q = 8
CCAP = 2
NCL = NB // AGG
PEERS = 128
DEST = NCL * S
PARTS = ((0, 8), (8, 19))
SIDE = 4
SHARES = 8
PIECES = 4
PAGE = 128
GROUP = 4
TILES = PEERS * Q // 2
LOCAL = NB + 2
GROUPS = 1024
POSITIONS = GROUPS * GROUP
CHUNK = 128
PITCH = 72
SPAN = Q // 2 * B
NOTE = 8
BATCH = 32
CHUNK_BITS = 7
BATCH_BITS = 5
STEPS = GROUPS // CHUNK
ROWS_STEP = 16
F32 = jnp.float32
BF16 = jnp.bfloat16


def low_lanes(shape):
    return lax.broadcasted_iota(jnp.int32, shape, 1) < B


def params(limit):
    return pltpu.CompilerParams(
        dimension_semantics=("arbitrary",), vmem_limit_bytes=limit * 1024 * 1024
    )


def pack_kernel(wanted, p_ref, send_hbm, local_hbm, staged, blocks, wide, sems):
    low = low_lanes((ROWS_STEP, L))

    def relayout(group, carry):
        row = pl.multiple_of(group * ROWS_STEP, ROWS_STEP)
        for m in range(B // 2):
            both = p_ref[pl.ds(row, ROWS_STEP), pl.ds(m * L, L)].astype(F32)
            turned = pltpu.roll(both, B, 1)
            even = jnp.where(low, both, turned)
            odd = jnp.where(low, turned, both)
            wide[pl.ds(2 * m, ROWS_STEP, stride=PITCH), :] = even
            wide[pl.ds(2 * m + 1, ROWS_STEP, stride=PITCH), :] = odd
        for g in range(ROWS_STEP):
            blocks[row + g] = wide[pl.ds(g * PITCH, B), :].astype(BF16)
        return carry

    lax.fori_loop(0, NB // ROWS_STEP, relayout, 0)
    zero = jnp.zeros((B, L), BF16)
    blocks[NB] = zero
    blocks[NB + 1] = zero
    left_half = low_lanes((B, L))
    share = PEERS // SHARES

    def fill(peer, carry):
        for u in range(Q // 2):
            first = wanted[2 * u, peer]
            second = wanted[2 * u + 1, peer]
            first = jnp.where(first < 0, NB, first)
            second = jnp.where(second < 0, NB, second)
            staged[peer, u * B : (u + 1) * B] = jnp.where(
                left_half, blocks[first], blocks[second]
            )
        return carry

    copies = []
    for n in range(SHARES):
        lax.fori_loop(n * share, (n + 1) * share, fill, 0, unroll=4)
        part = pl.ds(n * share, share)
        copies.append(pltpu.make_async_copy(staged.at[part], send_hbm.at[part], sems.at[n]))
        copies[-1].start()
    copies.append(pltpu.make_async_copy(blocks, local_hbm, sems.at[SHARES]))
    copies[-1].start()
    for copy in copies:
        copy.wait()


def pack(wanted, p_blocks):
    return pl.pallas_call(
        pack_kernel,
        grid_spec=pltpu.PrefetchScalarGridSpec(
            num_scalar_prefetch=1,
            grid=(1,),
            in_specs=[pl.BlockSpec((NB, B * B), lambda i, w: (0, 0))],
            out_specs=[pl.BlockSpec(memory_space=pl.ANY)] * 2,
            scratch_shapes=[
                pltpu.VMEM((PEERS, SPAN, L), BF16),
                pltpu.VMEM((LOCAL, B, L), BF16),
                pltpu.VMEM((ROWS_STEP * PITCH, L), F32),
                pltpu.SemaphoreType.DMA((SHARES + 1,)),
            ],
        ),
        out_shape=[
            jax.ShapeDtypeStruct((PEERS, SPAN, L), BF16),
            jax.ShapeDtypeStruct((LOCAL, B, L), BF16),
        ],
        compiler_params=params(60),
        name="pack",
    )(wanted, p_blocks)


def left_kernel(
    dest_in, code_in, a_ref, p_ref, sorted_hbm, code_ref, group_ref, count_ref,
    held, wide, turned_p, cursor, sem,
):
    step = pl.program_id(0)

    @pl.when(step == 0)
    def _():
        def clear(d, carry):
            cursor[d] = 0
            return carry

        lax.fori_loop(0, DEST, clear, 0, unroll=8)

        def count_of(k, carry):
            def count(row, carry):
                d = dest_in[k, row]
                cursor[d] = cursor[d] + 1
                return carry

            return lax.fori_loop(0, NB, count, carry, unroll=8)

        lax.fori_loop(0, K, count_of, 0)

        def place(d, at):
            here = cursor[d]
            cursor[d] = at
            return at + ((here + GROUP - 1) & -GROUP)

        at = 0
        for n, (start, width) in enumerate(PARTS):
            count_ref[2 * n] = at >> 2
            at = lax.fori_loop(start * NCL, (start + width) * NCL, place, at, unroll=8)
            count_ref[2 * n + 1] = at >> 2
            at = (at + GROUP * BATCH - 1) & -(GROUP * BATCH)

        def blank(i, carry):
            code_ref[i] = 2 * NB
            return carry

        lax.fori_loop(0, POSITIONS, blank, 0, unroll=16)

        def nowhere(i, carry):
            group_ref[i] = DEST
            return carry

        lax.fori_loop(0, GROUPS, nowhere, 0, unroll=16)
        zero = jnp.zeros((B, L), BF16)

        def wipe(i, carry):
            held[i] = zero
            return carry

        lax.fori_loop(0, 2 * GROUPS, wipe, 0, unroll=16)

    for g in range(ROWS_STEP):
        turned_p[g] = p_ref[g].astype(F32).T[:B].astype(BF16)

    low16 = low_lanes((ROWS_STEP, L))
    lane = lax.broadcasted_iota(jnp.int32, (B, L), 1)
    low = lane < B
    half = jnp.where(low, 0, 1)

    def insert(row, k, value, valid):
        d = dest_in[k, step * ROWS_STEP + row]
        at = cursor[d]
        cursor[d] = at + valid
        at = jnp.where(valid == 1, at, POSITIONS)
        code_ref[at] = code_in[k, step * ROWS_STEP + row]
        group_ref[at >> 2] = d
        tile = at >> 1
        held[tile] = jnp.where(half == (at & 1), value, held[tile].astype(F32)).astype(BF16)

    def pair_step(pair, carry):
        first = 2 * pair
        valid = jnp.where(first + 1 < K, 1, 0)
        second = jnp.minimum(first + 1, K - 1)
        for m in range(B // 2):
            one = a_ref[first, :, pl.ds(m * L, L)].astype(F32)
            two = a_ref[second, :, pl.ds(m * L, L)].astype(F32)
            wide[pl.ds(2 * m, ROWS_STEP, stride=PITCH), :] = jnp.where(
                low16, one, pltpu.roll(two, B, 1)
            )
            wide[pl.ds(2 * m + 1, ROWS_STEP, stride=PITCH), :] = jnp.where(
                low16, pltpu.roll(one, B, 1), two
            )
        for row in range(ROWS_STEP):
            block = wide[pl.ds(row * PITCH, B), :].astype(BF16)
            value = jnp.dot(turned_p[row], block, preferred_element_type=F32)
            turned = pltpu.roll(value, B, 1)
            insert(row, first, jnp.where(low, value, turned), 1)
            insert(row, second, jnp.where(low, turned, value), valid)
        return carry

    lax.fori_loop(0, (K + 1) // 2, pair_step, 0)

    @pl.when(step == pl.num_programs(0) - 1)
    def _():
        used = (2 * count_ref[2 * len(PARTS) - 1] + PAGE - 1) >> 7

        def page(n):
            at = pl.ds(pl.multiple_of(n * PAGE, PAGE), PAGE)
            return pltpu.make_async_copy(held.at[at], sorted_hbm.at[at], sem)

        def begin(n, carry):
            page(n).start()
            return carry

        def finish(n, carry):
            page(n).wait()
            return carry

        lax.fori_loop(0, used, begin, 0)
        lax.fori_loop(0, used, finish, 0)


def left(dest, code, a_turned, local):
    return pl.pallas_call(
        left_kernel,
        grid_spec=pltpu.PrefetchScalarGridSpec(
            num_scalar_prefetch=2,
            grid=(NB // ROWS_STEP,),
            in_specs=[
                pl.BlockSpec((K, ROWS_STEP, B * B), lambda i, *_: (0, i, 0)),
                pl.BlockSpec((ROWS_STEP, B, L), lambda i, *_: (i, 0, 0)),
            ],
            out_specs=[
                pl.BlockSpec(memory_space=pl.ANY),
                pl.BlockSpec(memory_space=pltpu.SMEM),
                pl.BlockSpec(memory_space=pltpu.SMEM),
                pl.BlockSpec(memory_space=pltpu.SMEM),
            ],
            scratch_shapes=[
                pltpu.VMEM((2 * GROUPS + 1, B, L), BF16),
                pltpu.VMEM((ROWS_STEP * PITCH, L), F32),
                pltpu.VMEM((ROWS_STEP, B, B), BF16),
                pltpu.SMEM((DEST,), jnp.int32),
                pltpu.SemaphoreType.DMA,
            ],
        ),
        out_shape=[
            jax.ShapeDtypeStruct((2 * GROUPS, B, L), BF16),
            jax.ShapeDtypeStruct((POSITIONS + GROUP,), jnp.int32),
            jax.ShapeDtypeStruct((GROUPS + 1,), jnp.int32),
            jax.ShapeDtypeStruct((2 * len(PARTS),), jnp.int32),
        ],
        compiler_params=params(56),
        cost_estimate=pl.CostEstimate(
            flops=2 * NB * K * B**3 * 16, bytes_accessed=60_000_000, transcendentals=0
        ),
        name="left",
    )(dest, code, a_turned, local)


def right_kernel(
    part, code_ref, group_ref, count_ref, bucket_ref, t_ref, local_hbm, ghost_hbm, out_hbm,
    blocks, total, wide, staged, halves, sems, out_sems,
):
    step = pl.program_id(0)
    start, width = PARTS[part]
    first = count_ref[2 * part]
    last = count_ref[2 * part + 1]
    origin = (first >> CHUNK_BITS) << CHUNK_BITS

    @pl.when(step == 0)
    def _():
        mine = pltpu.make_async_copy(local_hbm, blocks.at[pl.ds(0, LOCAL)], sems.at[0])
        piece = PEERS // PIECES
        others = [
            pltpu.make_async_copy(
                ghost_hbm.at[pl.ds(n * piece, piece)],
                blocks.at[pl.ds(LOCAL + n * piece * Q // 2, piece * Q // 2)].reshape(
                    piece, SPAN, L
                ),
                sems.at[n + 1],
            )
            for n in range(PIECES)
        ]
        for copy in others:
            copy.start()
        mine.start()
        low = low_lanes((16, L))
        halves[0] = jnp.where(low, 1.0, 0.0).astype(BF16)
        halves[1] = jnp.where(low, 0.0, 1.0).astype(BF16)
        zero = jnp.zeros((B, L), F32)

        def clear(i, carry):
            total[i] = zero
            return carry

        lax.fori_loop(0, width * NCL + 1, clear, 0, unroll=8)
        mine.wait()
        for copy in others:
            copy.wait()

    def batch(b, carry):
        for u in range(BATCH):
            here = b * BATCH + u
            group = origin + step * CHUNK + here
            lhs = jnp.concatenate([t_ref[2 * here], t_ref[2 * here + 1]], axis=1)
            parts = []
            for w in range(GROUP):
                code = code_ref[group * GROUP + w]
                block = blocks[code >> 1].reshape(B // 16, 16, L)
                parts.append((block * halves[code & 1][None]).reshape(B, L))
            rhs = jnp.concatenate(parts, axis=0)
            d = jnp.minimum(group_ref[group] - start * NCL, width * NCL)
            total[d] += jnp.dot(lhs, rhs, preferred_element_type=F32)
        return carry

    at = origin + step * CHUNK
    begin = jnp.clip((first - at) >> BATCH_BITS, 0, CHUNK // BATCH)
    end = jnp.clip((last - at + BATCH - 1) >> BATCH_BITS, 0, CHUNK // BATCH)
    lax.fori_loop(begin, end, batch, 0)

    @pl.when(step == STEPS - 1)
    def _():
        low = low_lanes((B // 2, L))
        copies = [
            pltpu.make_async_copy(staged.at[c], out_hbm.at[bucket_ref[c]], out_sems.at[c])
            for c in range(NCL)
        ]
        for c in range(NCL):

            def emit(s, carry, c=c):
                value = total[s * NCL + c]
                row = pl.multiple_of(s * B, B)
                wide[pl.ds(row, B), :] = value + pltpu.roll(value, B, 1)
                even = wide[pl.ds(row, B // 2, stride=2), :]
                odd = wide[pl.ds(row + 1, B // 2, stride=2), :]
                staged[c, s] = jnp.where(low, even, odd).astype(BF16)
                return carry

            lax.fori_loop(0, width, emit, 0, unroll=True)
            copies[c].start()
        for copy in copies:
            copy.wait()


def right(part, code, group, count, bucket, ordered, local, ghost, peers_y):
    width = PARTS[part][1]

    def t_map(i, code_ref, group_ref, count_ref, bucket_ref):
        block = (count_ref[2 * part] >> CHUNK_BITS) + i
        used = jnp.maximum(count_ref[2 * part + 1] - 1, 0) >> CHUNK_BITS
        return (jnp.minimum(block, used), 0, 0)

    return pl.pallas_call(
        functools.partial(right_kernel, part),
        grid_spec=pltpu.PrefetchScalarGridSpec(
            num_scalar_prefetch=4,
            grid=(STEPS,),
            in_specs=[
                pl.BlockSpec((2 * CHUNK, B, L), t_map),
                pl.BlockSpec(memory_space=pl.ANY),
                pl.BlockSpec(memory_space=pl.ANY),
            ],
            out_specs=pl.BlockSpec(memory_space=pl.ANY),
            scratch_shapes=[
                pltpu.VMEM((LOCAL + TILES, B, L), BF16),
                pltpu.VMEM((width * NCL + 1, B, L), F32),
                pltpu.VMEM((width * B, L), F32),
                pltpu.VMEM((NCL, width, B // 2, L), BF16),
                pltpu.VMEM((2, 16, L), BF16),
                pltpu.SemaphoreType.DMA((PIECES + 1,)),
                pltpu.SemaphoreType.DMA((NCL,)),
            ],
        ),
        out_shape=jax.ShapeDtypeStruct((peers_y * CCAP, width, B // 2, L), BF16),
        compiler_params=params(63),
        cost_estimate=pl.CostEstimate(
            flops=NB * K * B**3 * 32, bytes_accessed=30_000_000, transcendentals=0
        ),
        name="right%d" % part,
    )(code, group, count, bucket, ordered, local, ghost)


def exchange_kernel(x_ref, out_ref, send_sems, recv_sems, own_sem):
    px, me = lax.axis_index("px"), lax.axis_index("py")
    shifts = sorted(
        ((dx, dy) for dx in range(SIDE) for dy in range(SIDE) if dx or dy),
        key=lambda o: -min(o[0], SIDE - o[0]) - min(o[1], SIDE - o[1]),
    )

    def peer(shift):
        return (me // SIDE + shift[0]) % SIDE * SIDE + (me + shift[1]) % SIDE

    barrier = pltpu.get_barrier_semaphore()
    for shift in shifts:
        pl.semaphore_signal(
            barrier, inc=1, device_id=(px, peer(shift)), device_id_type=pl.DeviceIdType.MESH
        )
    pl.semaphore_wait(barrier, len(shifts))
    copies = []
    for n, shift in enumerate(shifts):
        copy = pltpu.make_async_remote_copy(
            src_ref=x_ref.at[peer(shift)],
            dst_ref=out_ref.at[me],
            send_sem=send_sems.at[n],
            recv_sem=recv_sems.at[n],
            device_id=(px, peer(shift)),
            device_id_type=pl.DeviceIdType.MESH,
        )
        copy.start()
        copies.append(copy)
    own = pltpu.make_async_copy(x_ref.at[me], out_ref.at[me], own_sem)
    own.start()
    own.wait()
    for copy in copies:
        copy.wait()


def exchange(rows, collective_id, name):
    peers = SIDE * SIDE
    return pl.pallas_call(
        exchange_kernel,
        in_specs=[pl.BlockSpec(memory_space=pl.ANY)],
        out_specs=pl.BlockSpec(memory_space=pl.ANY),
        out_shape=jax.ShapeDtypeStruct(rows.shape, rows.dtype),
        scratch_shapes=[
            pltpu.SemaphoreType.DMA((peers - 1,)),
            pltpu.SemaphoreType.DMA((peers - 1,)),
            pltpu.SemaphoreType.DMA,
        ],
        compiler_params=pltpu.CompilerParams(
            collective_id=collective_id, has_side_effects=True, vmem_limit_bytes=63 * 1024 * 1024
        ),
        cost_estimate=pl.CostEstimate(
            flops=0, bytes_accessed=300_000_000, transcendentals=0
        ),
        name=name,
    )(rows)


AHEAD = 4


def place_kernel(from_ref, *refs):
    ins, out_ref, wide = refs[:-2], refs[-2], refs[-1]
    step = pl.program_id(0)
    span = NCL * B // 2

    @pl.when(step < NCL // AHEAD)
    def _():
        for n, (start, width) in enumerate(PARTS):
            for j in range(AHEAD):
                rows = ins[n * AHEAD + j]

                def spread(s, carry, start=start, rows=rows, j=j):
                    at = (start + s) * span + step * AHEAD + j
                    wide[pl.ds(at, B // 2, stride=NCL), :] = rows[0, s].astype(F32)
                    return carry

                lax.fori_loop(0, width, spread, 0, unroll=True)

    @pl.when(step >= NCL // AHEAD)
    def _():
        def flatten(u, carry):
            start = pl.multiple_of(((step - NCL // AHEAD) * 9 + u) * span, span)
            for m in range(B // 2):
                out_ref[u, :, pl.ds(m * L, L)] = wide[
                    pl.ds(start + m * NCL, NCL), :
                ].astype(BF16)
            return carry

        lax.fori_loop(0, 9, flatten, 0)


def place(origin, arrived):
    turns = NCL // AHEAD

    def spec(width, j):
        return pl.BlockSpec(
            (1, width, B // 2, L),
            lambda i, o: (o[jnp.minimum(i, turns - 1) * AHEAD + j], 0, 0, 0),
        )

    return pl.pallas_call(
        place_kernel,
        grid_spec=pltpu.PrefetchScalarGridSpec(
            num_scalar_prefetch=1,
            grid=(turns + S // 9,),
            in_specs=[spec(width, j) for _, width in PARTS for j in range(AHEAD)],
            out_specs=pl.BlockSpec(
                (9, NCL, B * B), lambda i, o: (jnp.maximum(i - turns, 0), 0, 0)
            ),
            scratch_shapes=[pltpu.VMEM((S * NCL * B // 2, L), F32)],
        ),
        out_shape=jax.ShapeDtypeStruct((S, NCL, B * B), BF16),
        compiler_params=params(60),
        name="place",
    )(origin, *[rows for rows in arrived for _ in range(AHEAD)])


def lists(a_source, agg_local, coarse_slot):
    dest = (coarse_slot * NCL + agg_local[:, None]).T
    ghost = a_source - NB + 2 * LOCAL
    code = jnp.where(a_source < NB, 2 * a_source, ghost).T
    return dest, code


def buckets(targets, peers_y):
    column = targets // NCL % peers_y
    order = jnp.arange(NCL)
    same = column[:, :, None] == column[:, None, :]
    earlier = order[None, None, :] < order[None, :, None]
    rank = jnp.sum((same & earlier).astype(jnp.int32), axis=2)
    return (column * CCAP + rank).astype(jnp.int32)


def origins(targets, me):
    peers_y = targets.shape[0]
    order = jnp.arange(NCL)
    rank = buckets(targets, peers_y) % CCAP
    source = jnp.arange(peers_y)[:, None] * CCAP + rank
    here = (targets // NCL % peers_y == me)[:, :, None]
    here = here & ((targets % NCL)[:, :, None] == order[None, None, :])
    return jnp.sum(jnp.where(here, source[:, :, None], 0), axis=(0, 1)).astype(jnp.int32)


def body(a_blocks, p_blocks, a_source, send_list, agg_local, coarse_slot, coarse_target):
    peers_y = lax.axis_size("py")
    me = lax.axis_index("py")
    sending, local = pack(send_list.reshape(PEERS, Q).T, p_blocks)
    ghost = lax.all_to_all(sending, ("px", "py"), split_axis=0, concat_axis=0, tiled=True)
    bucket = buckets(coarse_target[None], peers_y)[0]
    dest, code = lists(a_source, agg_local, coarse_slot)
    ordered, code, group, count = left(dest, code, a_blocks.transpose(1, 0, 2), local)
    tied, _ = lax.optimization_barrier((coarse_target, count))
    note = jnp.broadcast_to(jnp.pad(tied, (0, L - NCL)), (peers_y, NOTE, L))
    targets = exchange(note, 1, "targets")
    origin = origins(targets[:, 0, :NCL], me)
    bucket = jnp.concatenate([bucket, origin])
    arrived = []
    for part, (_, width) in enumerate(PARTS):
        formed = right(part, code, group, count, bucket, ordered, local, ghost, peers_y)
        rows = formed.reshape(peers_y, CCAP * width * B // 2, L)
        if part == 0:
            rows = lax.all_to_all(rows, "py", split_axis=0, concat_axis=0, tiled=True)
        else:
            rows = exchange(rows, 0, "exchange")
        arrived.append(rows.reshape(peers_y * CCAP, width, B // 2, L))
    return place(origin, arrived).transpose(1, 0, 2)


def solution(mesh):
    both = ("px", "py")
    in_specs = (
        P(both, None, None), P(both, None), P(both, None), P(both, None, None), P(both),
        P(both, None), P(both),
    )
    return jax.shard_map(
        body, mesh=mesh, in_specs=in_specs, out_specs=P(both, None, None), check_vma=False
    )
```

```python
import functools

import jax
import jax.numpy as jnp
from jax import lax
from jax.experimental import pallas as pl
from jax.experimental.pallas import tpu as pltpu
from jax.sharding import PartitionSpec as P

B = 64
L = 2 * B
NB = 96
K = 27
S = 27
AGG = 6
Q = 8
CCAP = 2
NCL = NB // AGG
PEERS = 128
DEST = NCL * S
PARTS = ((0, 9), (9, 18))
COUNTERS = 4
SIDE = 4
SHARES = 8
PIECES = 4
PAGE = 128
GROUP = 4
TILES = PEERS * Q // 2
LOCAL = NB + 2
GROUPS = 1024
POSITIONS = GROUPS * GROUP
CHUNK = 128
PITCH = 72
SPAN = Q // 2 * B
NOTE = 8
BATCH = 32
CHUNK_BITS = 7
BATCH_BITS = 5
STEPS = GROUPS // CHUNK
ROWS_STEP = 16
F32 = jnp.float32
BF16 = jnp.bfloat16


def low_lanes(shape):
    return lax.broadcasted_iota(jnp.int32, shape, 1) < B


def params(limit):
    return pltpu.CompilerParams(
        dimension_semantics=("arbitrary",), vmem_limit_bytes=limit * 1024 * 1024
    )


def pack_kernel(wanted, p_ref, send_hbm, local_hbm, staged, blocks, wide, sems):
    low = low_lanes((ROWS_STEP, L))

    def relayout(group, carry):
        row = pl.multiple_of(group * ROWS_STEP, ROWS_STEP)
        for m in range(B // 2):
            both = p_ref[pl.ds(row, ROWS_STEP), pl.ds(m * L, L)].astype(F32)
            turned = pltpu.roll(both, B, 1)
            even = jnp.where(low, both, turned)
            odd = jnp.where(low, turned, both)
            wide[pl.ds(2 * m, ROWS_STEP, stride=PITCH), :] = even
            wide[pl.ds(2 * m + 1, ROWS_STEP, stride=PITCH), :] = odd
        for g in range(ROWS_STEP):
            blocks[row + g] = wide[pl.ds(g * PITCH, B), :].astype(BF16)
        return carry

    lax.fori_loop(0, NB // ROWS_STEP, relayout, 0)
    zero = jnp.zeros((B, L), BF16)
    blocks[NB] = zero
    blocks[NB + 1] = zero
    left_half = low_lanes((B, L))
    share = PEERS // SHARES

    def fill(peer, carry):
        for u in range(Q // 2):
            first = wanted[2 * u, peer]
            second = wanted[2 * u + 1, peer]
            first = jnp.where(first < 0, NB, first)
            second = jnp.where(second < 0, NB, second)
            staged[peer, u * B : (u + 1) * B] = jnp.where(
                left_half, blocks[first], blocks[second]
            )
        return carry

    copies = []
    for n in range(SHARES):
        lax.fori_loop(n * share, (n + 1) * share, fill, 0, unroll=4)
        part = pl.ds(n * share, share)
        copies.append(pltpu.make_async_copy(staged.at[part], send_hbm.at[part], sems.at[n]))
        copies[-1].start()
    copies.append(pltpu.make_async_copy(blocks, local_hbm, sems.at[SHARES]))
    copies[-1].start()
    for copy in copies:
        copy.wait()


def pack(wanted, p_blocks):
    return pl.pallas_call(
        pack_kernel,
        grid_spec=pltpu.PrefetchScalarGridSpec(
            num_scalar_prefetch=1,
            grid=(1,),
            in_specs=[pl.BlockSpec((NB, B * B), lambda i, w: (0, 0))],
            out_specs=[pl.BlockSpec(memory_space=pl.ANY)] * 2,
            scratch_shapes=[
                pltpu.VMEM((PEERS, SPAN, L), BF16),
                pltpu.VMEM((LOCAL, B, L), BF16),
                pltpu.VMEM((ROWS_STEP * PITCH, L), F32),
                pltpu.SemaphoreType.DMA((SHARES + 1,)),
            ],
        ),
        out_shape=[
            jax.ShapeDtypeStruct((PEERS, SPAN, L), BF16),
            jax.ShapeDtypeStruct((LOCAL, B, L), BF16),
        ],
        compiler_params=params(60),
        name="pack",
    )(wanted, p_blocks)


def left_kernel(
    dest_in, code_in, a_ref, p_ref, sorted_hbm, code_ref, group_ref, count_ref,
    held, wide, turned_p, cursor, *rest,
):
    counters, sem = (cursor, *rest[:-1]), rest[-1]
    step = pl.program_id(0)

    @pl.when(step == 0)
    def _():
        def clear(d, carry):
            for counter in counters:
                counter[d] = 0
            return carry

        lax.fori_loop(0, DEST, clear, 0, unroll=8)

        def count_of(k, carry):
            def count(row, carry):
                for n, counter in enumerate(counters):
                    d = dest_in[k, n * (NB // COUNTERS) + row]
                    counter[d] = counter[d] + 1
                return carry

            return lax.fori_loop(0, NB // COUNTERS, count, carry, unroll=8)

        lax.fori_loop(0, K, count_of, 0)

        def place(d, at):
            here = sum(counter[d] for counter in counters)
            cursor[d] = at
            return at + ((here + GROUP - 1) & -GROUP)

        at = 0
        for n, (start, width) in enumerate(PARTS):
            count_ref[2 * n] = at >> 2
            at = lax.fori_loop(start * NCL, (start + width) * NCL, place, at, unroll=8)
            count_ref[2 * n + 1] = at >> 2
            at = (at + GROUP * BATCH - 1) & -(GROUP * BATCH)

        def blank(i, carry):
            code_ref[i] = 2 * NB
            return carry

        lax.fori_loop(0, POSITIONS, blank, 0, unroll=16)

        def nowhere(i, carry):
            group_ref[i] = DEST
            return carry

        lax.fori_loop(0, GROUPS, nowhere, 0, unroll=16)
        zero = jnp.zeros((B, L), BF16)

        def wipe(i, carry):
            held[i] = zero
            return carry

        lax.fori_loop(0, 2 * GROUPS, wipe, 0, unroll=16)

    for g in range(ROWS_STEP):
        turned_p[g] = p_ref[g].astype(F32).T[:B].astype(BF16)

    low16 = low_lanes((ROWS_STEP, L))
    lane = lax.broadcasted_iota(jnp.int32, (B, L), 1)
    low = lane < B
    half = jnp.where(low, 0, 1)

    def insert(row, k, value, valid):
        d = dest_in[k, step * ROWS_STEP + row]
        at = cursor[d]
        cursor[d] = at + valid
        at = jnp.where(valid == 1, at, POSITIONS)
        code_ref[at] = code_in[k, step * ROWS_STEP + row]
        group_ref[at >> 2] = d
        tile = at >> 1
        held[tile] = jnp.where(half == (at & 1), value, held[tile].astype(F32)).astype(BF16)

    def pair_step(pair, carry):
        first = 2 * pair
        valid = jnp.where(first + 1 < K, 1, 0)
        second = jnp.minimum(first + 1, K - 1)
        for m in range(B // 2):
            one = a_ref[first, :, pl.ds(m * L, L)].astype(F32)
            two = a_ref[second, :, pl.ds(m * L, L)].astype(F32)
            wide[pl.ds(2 * m, ROWS_STEP, stride=PITCH), :] = jnp.where(
                low16, one, pltpu.roll(two, B, 1)
            )
            wide[pl.ds(2 * m + 1, ROWS_STEP, stride=PITCH), :] = jnp.where(
                low16, pltpu.roll(one, B, 1), two
            )
        for row in range(ROWS_STEP):
            block = wide[pl.ds(row * PITCH, B), :].astype(BF16)
            value = jnp.dot(turned_p[row], block, preferred_element_type=F32)
            turned = pltpu.roll(value, B, 1)
            insert(row, first, jnp.where(low, value, turned), 1)
            insert(row, second, jnp.where(low, turned, value), valid)
        return carry

    lax.fori_loop(0, (K + 1) // 2, pair_step, 0)

    @pl.when(step == pl.num_programs(0) - 1)
    def _():
        used = (2 * count_ref[2 * len(PARTS) - 1] + PAGE - 1) >> 7

        def page(n):
            at = pl.ds(pl.multiple_of(n * PAGE, PAGE), PAGE)
            return pltpu.make_async_copy(held.at[at], sorted_hbm.at[at], sem)

        def begin(n, carry):
            page(n).start()
            return carry

        def finish(n, carry):
            page(n).wait()
            return carry

        lax.fori_loop(0, used, begin, 0)
        lax.fori_loop(0, used, finish, 0)


def left(dest, code, a_turned, local):
    return pl.pallas_call(
        left_kernel,
        grid_spec=pltpu.PrefetchScalarGridSpec(
            num_scalar_prefetch=2,
            grid=(NB // ROWS_STEP,),
            in_specs=[
                pl.BlockSpec((K, ROWS_STEP, B * B), lambda i, *_: (0, i, 0)),
                pl.BlockSpec((ROWS_STEP, B, L), lambda i, *_: (i, 0, 0)),
            ],
            out_specs=[
                pl.BlockSpec(memory_space=pl.ANY),
                pl.BlockSpec(memory_space=pltpu.SMEM),
                pl.BlockSpec(memory_space=pltpu.SMEM),
                pl.BlockSpec(memory_space=pltpu.SMEM),
            ],
            scratch_shapes=[
                pltpu.VMEM((2 * GROUPS + 1, B, L), BF16),
                pltpu.VMEM((ROWS_STEP * PITCH, L), F32),
                pltpu.VMEM((ROWS_STEP, B, B), BF16),
                *[pltpu.SMEM((DEST,), jnp.int32) for _ in range(COUNTERS)],
                pltpu.SemaphoreType.DMA,
            ],
        ),
        out_shape=[
            jax.ShapeDtypeStruct((2 * GROUPS, B, L), BF16),
            jax.ShapeDtypeStruct((POSITIONS + GROUP,), jnp.int32),
            jax.ShapeDtypeStruct((GROUPS + 1,), jnp.int32),
            jax.ShapeDtypeStruct((2 * len(PARTS),), jnp.int32),
        ],
        compiler_params=params(56),
        cost_estimate=pl.CostEstimate(
            flops=2 * NB * K * B**3 * 16, bytes_accessed=60_000_000, transcendentals=0
        ),
        name="left",
    )(dest, code, a_turned, local)


def right_kernel(
    part, code_ref, group_ref, count_ref, bucket_ref, t_ref, local_hbm, ghost_hbm, out_hbm,
    blocks, total, wide, staged, halves, sems, out_sems,
):
    step = pl.program_id(0)
    start, width = PARTS[part]
    first = count_ref[2 * part]
    last = count_ref[2 * part + 1]
    origin = (first >> CHUNK_BITS) << CHUNK_BITS

    @pl.when(step == 0)
    def _():
        mine = pltpu.make_async_copy(local_hbm, blocks.at[pl.ds(0, LOCAL)], sems.at[0])
        piece = PEERS // PIECES
        others = [
            pltpu.make_async_copy(
                ghost_hbm.at[pl.ds(n * piece, piece)],
                blocks.at[pl.ds(LOCAL + n * piece * Q // 2, piece * Q // 2)].reshape(
                    piece, SPAN, L
                ),
                sems.at[n + 1],
            )
            for n in range(PIECES)
        ]
        for copy in others:
            copy.start()
        mine.start()
        low = low_lanes((16, L))
        halves[0] = jnp.where(low, 1.0, 0.0).astype(BF16)
        halves[1] = jnp.where(low, 0.0, 1.0).astype(BF16)
        zero = jnp.zeros((B, L), F32)

        def clear(i, carry):
            total[i] = zero
            return carry

        lax.fori_loop(0, width * NCL + 1, clear, 0, unroll=8)
        mine.wait()
        for copy in others:
            copy.wait()

    def batch(b, carry):
        for u in range(BATCH):
            here = b * BATCH + u
            group = origin + step * CHUNK + here
            lhs = jnp.concatenate([t_ref[2 * here], t_ref[2 * here + 1]], axis=1)
            parts = []
            for w in range(GROUP):
                code = code_ref[group * GROUP + w]
                block = blocks[code >> 1].reshape(B // 16, 16, L)
                parts.append((block * halves[code & 1][None]).reshape(B, L))
            rhs = jnp.concatenate(parts, axis=0)
            d = jnp.minimum(group_ref[group] - start * NCL, width * NCL)
            total[d] += jnp.dot(lhs, rhs, preferred_element_type=F32)
        return carry

    at = origin + step * CHUNK
    begin = jnp.clip((first - at) >> BATCH_BITS, 0, CHUNK // BATCH)
    end = jnp.clip((last - at + BATCH - 1) >> BATCH_BITS, 0, CHUNK // BATCH)
    lax.fori_loop(begin, end, batch, 0)

    @pl.when(step == STEPS - 1)
    def _():
        low = low_lanes((B // 2, L))
        copies = [
            pltpu.make_async_copy(staged.at[c], out_hbm.at[bucket_ref[c]], out_sems.at[c])
            for c in range(NCL)
        ]
        for c in range(NCL):

            def emit(s, carry, c=c):
                value = total[s * NCL + c]
                row = pl.multiple_of(s * B, B)
                wide[pl.ds(row, B), :] = value + pltpu.roll(value, B, 1)
                even = wide[pl.ds(row, B // 2, stride=2), :]
                odd = wide[pl.ds(row + 1, B // 2, stride=2), :]
                staged[c, s] = jnp.where(low, even, odd).astype(BF16)
                return carry

            lax.fori_loop(0, width, emit, 0, unroll=True)
            copies[c].start()
        for copy in copies:
            copy.wait()


def right(part, code, group, count, bucket, ordered, local, ghost, peers_y):
    width = PARTS[part][1]

    def t_map(i, code_ref, group_ref, count_ref, bucket_ref):
        block = (count_ref[2 * part] >> CHUNK_BITS) + i
        used = jnp.maximum(count_ref[2 * part + 1] - 1, 0) >> CHUNK_BITS
        return (jnp.minimum(block, used), 0, 0)

    return pl.pallas_call(
        functools.partial(right_kernel, part),
        grid_spec=pltpu.PrefetchScalarGridSpec(
            num_scalar_prefetch=4,
            grid=(STEPS,),
            in_specs=[
                pl.BlockSpec((2 * CHUNK, B, L), t_map),
                pl.BlockSpec(memory_space=pl.ANY),
                pl.BlockSpec(memory_space=pl.ANY),
            ],
            out_specs=pl.BlockSpec(memory_space=pl.ANY),
            scratch_shapes=[
                pltpu.VMEM((LOCAL + TILES, B, L), BF16),
                pltpu.VMEM((width * NCL + 1, B, L), F32),
                pltpu.VMEM((width * B, L), F32),
                pltpu.VMEM((NCL, width, B // 2, L), BF16),
                pltpu.VMEM((2, 16, L), BF16),
                pltpu.SemaphoreType.DMA((PIECES + 1,)),
                pltpu.SemaphoreType.DMA((NCL,)),
            ],
        ),
        out_shape=jax.ShapeDtypeStruct((peers_y * CCAP, width, B // 2, L), BF16),
        compiler_params=params(63),
        cost_estimate=pl.CostEstimate(
            flops=NB * K * B**3 * 32, bytes_accessed=30_000_000, transcendentals=0
        ),
        name="right%d" % part,
    )(code, group, count, bucket, ordered, local, ghost)


def exchange_kernel(x_ref, out_ref, send_sems, recv_sems, own_sem):
    px, me = lax.axis_index("px"), lax.axis_index("py")
    shifts = sorted(
        ((dx, dy) for dx in range(SIDE) for dy in range(SIDE) if dx or dy),
        key=lambda o: -min(o[0], SIDE - o[0]) - min(o[1], SIDE - o[1]),
    )

    def peer(shift):
        return (me // SIDE + shift[0]) % SIDE * SIDE + (me + shift[1]) % SIDE

    barrier = pltpu.get_barrier_semaphore()
    for shift in shifts:
        pl.semaphore_signal(
            barrier, inc=1, device_id=(px, peer(shift)), device_id_type=pl.DeviceIdType.MESH
        )
    pl.semaphore_wait(barrier, len(shifts))
    copies = []
    for n, shift in enumerate(shifts):
        copy = pltpu.make_async_remote_copy(
            src_ref=x_ref.at[peer(shift)],
            dst_ref=out_ref.at[me],
            send_sem=send_sems.at[n],
            recv_sem=recv_sems.at[n],
            device_id=(px, peer(shift)),
            device_id_type=pl.DeviceIdType.MESH,
        )
        copy.start()
        copies.append(copy)
    own = pltpu.make_async_copy(x_ref.at[me], out_ref.at[me], own_sem)
    own.start()
    own.wait()
    for copy in copies:
        copy.wait()


def exchange(rows, collective_id, name):
    peers = SIDE * SIDE
    return pl.pallas_call(
        exchange_kernel,
        in_specs=[pl.BlockSpec(memory_space=pl.ANY)],
        out_specs=pl.BlockSpec(memory_space=pl.ANY),
        out_shape=jax.ShapeDtypeStruct(rows.shape, rows.dtype),
        scratch_shapes=[
            pltpu.SemaphoreType.DMA((peers - 1,)),
            pltpu.SemaphoreType.DMA((peers - 1,)),
            pltpu.SemaphoreType.DMA,
        ],
        compiler_params=pltpu.CompilerParams(
            collective_id=collective_id, has_side_effects=True, vmem_limit_bytes=63 * 1024 * 1024
        ),
        cost_estimate=pl.CostEstimate(
            flops=0, bytes_accessed=300_000_000, transcendentals=0
        ),
        name=name,
    )(rows)


AHEAD = 4


def place_kernel(from_ref, *refs):
    ins, out_ref, wide = refs[:-2], refs[-2], refs[-1]
    step = pl.program_id(0)
    span = NCL * B // 2

    @pl.when(step < NCL // AHEAD)
    def _():
        for n, (start, width) in enumerate(PARTS):
            for j in range(AHEAD):
                rows = ins[n * AHEAD + j]

                def spread(s, carry, start=start, rows=rows, j=j):
                    at = (start + s) * span + step * AHEAD + j
                    wide[pl.ds(at, B // 2, stride=NCL), :] = rows[0, s].astype(F32)
                    return carry

                lax.fori_loop(0, width, spread, 0, unroll=True)

    @pl.when(step >= NCL // AHEAD)
    def _():
        def flatten(u, carry):
            start = pl.multiple_of(((step - NCL // AHEAD) * 9 + u) * span, span)
            for m in range(B // 2):
                out_ref[u, :, pl.ds(m * L, L)] = wide[
                    pl.ds(start + m * NCL, NCL), :
                ].astype(BF16)
            return carry

        lax.fori_loop(0, 9, flatten, 0)


def place(origin, arrived):
    turns = NCL // AHEAD

    def spec(width, j):
        return pl.BlockSpec(
            (1, width, B // 2, L),
            lambda i, o: (o[jnp.minimum(i, turns - 1) * AHEAD + j], 0, 0, 0),
        )

    return pl.pallas_call(
        place_kernel,
        grid_spec=pltpu.PrefetchScalarGridSpec(
            num_scalar_prefetch=1,
            grid=(turns + S // 9,),
            in_specs=[spec(width, j) for _, width in PARTS for j in range(AHEAD)],
            out_specs=pl.BlockSpec(
                (9, NCL, B * B), lambda i, o: (jnp.maximum(i - turns, 0), 0, 0)
            ),
            scratch_shapes=[pltpu.VMEM((S * NCL * B // 2, L), F32)],
        ),
        out_shape=jax.ShapeDtypeStruct((S, NCL, B * B), BF16),
        compiler_params=params(60),
        name="place",
    )(origin, *[rows for rows in arrived for _ in range(AHEAD)])


def lists(a_source, agg_local, coarse_slot):
    dest = (coarse_slot * NCL + agg_local[:, None]).T
    ghost = a_source - NB + 2 * LOCAL
    code = jnp.where(a_source < NB, 2 * a_source, ghost).T
    return dest, code


def buckets(targets, peers_y):
    column = targets // NCL % peers_y
    order = jnp.arange(NCL)
    same = column[:, :, None] == column[:, None, :]
    earlier = order[None, None, :] < order[None, :, None]
    rank = jnp.sum((same & earlier).astype(jnp.int32), axis=2)
    return (column * CCAP + rank).astype(jnp.int32)


def origins(targets, me):
    peers_y = targets.shape[0]
    order = jnp.arange(NCL)
    rank = buckets(targets, peers_y) % CCAP
    source = jnp.arange(peers_y)[:, None] * CCAP + rank
    here = (targets // NCL % peers_y == me)[:, :, None]
    here = here & ((targets % NCL)[:, :, None] == order[None, None, :])
    return jnp.sum(jnp.where(here, source[:, :, None], 0), axis=(0, 1)).astype(jnp.int32)


def body(a_blocks, p_blocks, a_source, send_list, agg_local, coarse_slot, coarse_target):
    peers_y = lax.axis_size("py")
    me = lax.axis_index("py")
    sending, local = pack(send_list.reshape(PEERS, Q).T, p_blocks)
    ghost = lax.all_to_all(sending, ("px", "py"), split_axis=0, concat_axis=0, tiled=True)
    bucket = buckets(coarse_target[None], peers_y)[0]
    dest, code = lists(a_source, agg_local, coarse_slot)
    ordered, code, group, count = left(dest, code, a_blocks.transpose(1, 0, 2), local)
    tied, _ = lax.optimization_barrier((coarse_target, count))
    note = jnp.broadcast_to(jnp.pad(tied, (0, L - NCL)), (peers_y, NOTE, L))
    targets = exchange(note, 1, "targets")
    origin = origins(targets[:, 0, :NCL], me)
    bucket = jnp.concatenate([bucket, origin])
    arrived = []
    for part, (_, width) in enumerate(PARTS):
        formed = right(part, code, group, count, bucket, ordered, local, ghost, peers_y)
        rows = formed.reshape(peers_y, CCAP * width * B // 2, L)
        if part == 0:
            rows = lax.all_to_all(rows, "py", split_axis=0, concat_axis=0, tiled=True)
        else:
            rows = exchange(rows, 0, "exchange")
        arrived.append(rows.reshape(peers_y * CCAP, width, B // 2, L))
    return place(origin, arrived).transpose(1, 0, 2)


def solution(mesh):
    both = ("px", "py")
    in_specs = (
        P(both, None, None), P(both, None), P(both, None), P(both, None, None), P(both),
        P(both, None), P(both),
    )
    return jax.shard_map(
        body, mesh=mesh, in_specs=in_specs, out_specs=P(both, None, None), check_vma=False
    )
```
